256 devices in a mesh: chan: 16 (over y, x), row: 4 (over z_lo), col: 4 (over z_hi, core).
Axes of the slice: x: 4, y: 4, z: 8 (z_hi: 2, z_lo: 4; z = z_hi * 4 + z_lo), core: 2. Of those that a mesh axis runs over, the one named last changes fastest.
Arguments:
- voltages: bfloat16 [2, 2048, 265216], P(None, ('row', 'col', 'chan')), may hold values from -6 to 6
- fir_window: float32 [4, 1024], replicated, may hold values from 0.5 to 1.5
- flags: int32 [2048, 256], P(('row', 'col', 'chan')), may hold values 0 or 1
Outputs:
- visibility: float32 [2, 32, 2048, 4, 512], P(None, 'chan', 'row', None, 'col')
The draws below stay inside these ranges and needn't reach their ends.
All inputs are finite; a program needn't handle non-finite values. No bound on the sum of `flags` on one device may be relied on, other than what follows from the above.
Results may differ from the reference program's by a relative error of at most 0.0039.
Values may be sent and summed in bfloat16 or wider, within the bound.
A program may use at most 128 MiB of HBM per device.

```python
import math
import jax
import jax.numpy as jnp
from jax import lax

ANTENNA_COUNT = 2048
CHANNEL_COUNT = 1024
FILTER_TAPS = 4
SPECTRA_COUNT = 256
BAND_CHANNELS = 32
SAMPLE_COUNT = 265216
N_ROW = 4


def with_ends(entries, rng, least, high):
    spot = [jax.random.randint(jax.random.fold_in(rng, axis), (), 0, length) for axis, length in enumerate(entries.shape)]
    longest = entries.shape.index(max(entries.shape))
    neighbour = spot[:longest] + [(spot[longest] + 1) % entries.shape[longest]] + spot[longest + 1:]
    return entries.at[tuple(spot)].set(least).at[tuple(neighbour)].set(high)


def block_scale(stream_key, shape, pieces, least, top_value):
    loudness, own = 1.0, jax.random.fold_in(stream_key, 6)
    for axis_at, blocks in pieces:
        heights = jnp.exp(jax.random.uniform(jax.random.fold_in(own, axis_at), (blocks,), jnp.float32, least / len(pieces), top_value / len(pieces)))
        loudness = loudness * jnp.repeat(heights, shape[axis_at] // blocks).reshape([-1 if axis == axis_at else 1 for axis in range(len(shape))])
    return loudness


def centred(rng, extent, width, bound, shards=(), kind=jnp.bfloat16):
    factor_of = block_scale(rng, extent, shards, -0.22, 0.18) if shards else 1.0
    result = jax.random.normal(rng, extent, jnp.float32) * width * factor_of
    return jnp.minimum(jnp.maximum(result, -bound), bound).astype(kind)


def setup_inputs(seed: int = 0) -> dict:
    keys = jax.random.split(jax.random.key(seed), 4)
    return {
        "voltages": centred(keys[0], (2, ANTENNA_COUNT, SAMPLE_COUNT), 1.0, 6.0, ((1, 256),)),
        "fir_window": jnp.clip(jax.random.uniform(keys[1], (FILTER_TAPS, CHANNEL_COUNT), jnp.float32, 0.5, 1.5), 0.5, 1.5),
        "flags": with_ends((jax.random.randint(keys[2], (ANTENNA_COUNT, SPECTRA_COUNT), 0, 8) < 7).astype(jnp.int32), jax.random.fold_in(keys[2], 1), 0, 1),
    }


def build_table(fir_window, band_total):
    chan_index = jnp.arange(CHANNEL_COUNT, dtype=jnp.int32)
    band_index = jnp.arange(band_total, dtype=jnp.int32)
    phase_index = chan_index[:, None] * band_index[None, :] % CHANNEL_COUNT
    angles = phase_index.astype(jnp.float32) * (2.0 * math.pi / CHANNEL_COUNT)
    weighting = fir_window / math.sqrt(FILTER_TAPS * CHANNEL_COUNT)
    cosine = (weighting[:, :, None] * jnp.cos(angles)[None]).astype(jnp.bfloat16)
    sine_part = (weighting[:, :, None] * jnp.sin(angles)[None]).astype(jnp.bfloat16)
    return (cosine, sine_part)

def reference(voltages, fir_window, flags):
    cosine, sine_part = build_table(fir_window, BAND_CHANNELS)
    cos_wide = cosine.astype(jnp.float32)
    sin_wide = sine_part.astype(jnp.float32)
    channel_group = ANTENNA_COUNT // 16
    high = lax.Precision.HIGHEST

    def one_group(index):
        piece = lax.dynamic_slice_in_dim(voltages, index * channel_group, channel_group, 1).astype(jnp.float32)
        filter_frames = piece.reshape(2, channel_group, SPECTRA_COUNT + FILTER_TAPS - 1, CHANNEL_COUNT)
        mask_piece = lax.dynamic_slice_in_dim(flags, index * channel_group, channel_group, 0).astype(jnp.float32)
        real_sum = jnp.zeros((BAND_CHANNELS, channel_group, SPECTRA_COUNT), jnp.float32)
        imag_sum = jnp.zeros((BAND_CHANNELS, channel_group, SPECTRA_COUNT), jnp.float32)
        for tap in range(FILTER_TAPS):
            window_real = filter_frames[0, :, tap:tap + SPECTRA_COUNT]
            window_imag = filter_frames[1, :, tap:tap + SPECTRA_COUNT]
            real_sum = real_sum + jnp.einsum('gsn,nk->kgs', window_real, cos_wide[tap], precision=high) + jnp.einsum('gsn,nk->kgs', window_imag, sin_wide[tap], precision=high)
            imag_sum = imag_sum + jnp.einsum('gsn,nk->kgs', window_imag, cos_wide[tap], precision=high) - jnp.einsum('gsn,nk->kgs', window_real, sin_wide[tap], precision=high)
        return jnp.stack([real_sum, imag_sum]) * mask_piece[None, None]
    sample_blocks = lax.map(one_group, jnp.arange(16, dtype=jnp.int32))
    spectra_rows = sample_blocks.transpose(1, 2, 0, 3, 4).reshape(2, BAND_CHANNELS, ANTENNA_COUNT, SPECTRA_COUNT)
    spectra_rows = spectra_rows.astype(jnp.bfloat16).astype(jnp.float32)

    def one_channel(index):
        chan_real = spectra_rows[0, index]
        chan_imag = spectra_rows[1, index]
        real_part = jnp.dot(chan_real, chan_real.T, precision=high) + jnp.dot(chan_imag, chan_imag.T, precision=high)
        imag_part = jnp.dot(chan_imag, chan_real.T, precision=high) - jnp.dot(chan_real, chan_imag.T, precision=high)
        return jnp.stack([real_part, imag_part]) * (1.0 / math.sqrt(SPECTRA_COUNT))
    cross_output = lax.map(one_channel, jnp.arange(BAND_CHANNELS, dtype=jnp.int32))
    return cross_output.transpose(1, 0, 2, 3).reshape(2, BAND_CHANNELS, ANTENNA_COUNT, N_ROW, ANTENNA_COUNT // N_ROW)
```

```python
import functools
import math

import jax
import jax.numpy as jnp
import numpy as np
from jax import lax
from jax.experimental import pallas as pl
from jax.experimental.pallas import tpu as pltpu
from jax.sharding import PartitionSpec as P

MESH = pl.DeviceIdType.MESH

CHANNELS = 1024
TAPS = 4
BAND = 32
SPECTRA = 256
FRAMES = SPECTRA + TAPS - 1
ANT = 8
GROUPS = 16
PER = BAND // GROUPS
N_ROW = 4
PLANES = 8
CHUNKS = 2
WIDTH = SPECTRA // CHUNKS
BOUNDS = (0, 132, FRAMES)
BLOCK = 44
PADDED = 264

PLAN = {
    0: [(0, 0, 1, False), (0, 3, -1, True), (0, 2, -2, True), (1, 0, 1, False), (1, 3, -1, True), (1, 2, -2, True)],
    1: [
        (0, 1, 1, False), (0, 1, -1, False), (0, 0, 1, False), (0, 2, -1, False), (0, 3, -1, False),
        (1, 1, 1, False), (1, 1, -1, False), (1, 0, 1, False), (1, 2, -1, False), (1, 3, -1, False),
    ],
    2: [
        (0, 2, -1, False), (0, 2, 1, False), (0, 3, -1, False), (0, 1, 1, False), (0, 0, 1, False),
        (1, 2, -1, False), (1, 2, 1, False), (1, 3, -1, False), (1, 1, 1, False), (1, 0, 1, False),
    ],
    3: [(0, 3, -1, False), (0, 0, 1, True), (0, 1, 2, True), (1, 3, -1, False), (1, 0, 1, True), (1, 1, 2, True)],
}


def basis():
    n = np.arange(CHANNELS)[:, None]
    k = np.arange(BAND)[None, :]
    angle = ((n * k) % CHANNELS).astype(np.float32) * np.float32(2.0 * math.pi / CHANNELS)
    cos, sin = np.cos(angle), np.sin(angle)
    return np.stack([np.concatenate([cos, -sin], 1), np.concatenate([sin, cos], 1)])


def gather_kernel(
    volt, table, flags, rows, cols,
    vbuf, gbuf, cbuf, tbuf, sbuf,
    volt_sem, turn_send, turn_recv, own_sem, line_send, row_recv, col_recv, swap_send,
):
    k = lax.axis_index("chan")
    r = lax.axis_index("row")
    c = lax.axis_index("col")
    hi, core = c // 2, c % 2
    plane = hi * N_ROW + r
    other = 1 - core

    def at_plane(offset):
        z = (plane + offset + PLANES) % PLANES
        return (k, z % N_ROW, (z // N_ROW) * 2 + core)

    mate = (k, r, hi * 2 + other)

    reads = []
    for chunk in range(CHUNKS):
        lo, up = BOUNDS[chunk], BOUNDS[chunk + 1]
        copy = pltpu.make_async_copy(
            volt.at[:, pl.ds(lo, up - lo)], vbuf.at[:, pl.ds(lo, up - lo)], volt_sem.at[chunk]
        )
        copy.start()
        reads.append(copy)

    barrier = pltpu.get_barrier_semaphore()

    def greet(d, carry):
        pl.semaphore_signal(barrier, inc=1, device_id=((k + d) % GROUPS, r, c), device_id_type=MESH)
        return carry

    lax.fori_loop(1, GROUPS, greet, 0)
    for offset in (-2, -1, 1, 2):
        pl.semaphore_signal(barrier, inc=1, device_id=at_plane(offset), device_id_type=MESH)
    pl.semaphore_signal(barrier, inc=1, device_id=mate, device_id_type=MESH)

    def channelise(chunk):
        lo, up = BOUNDS[chunk], BOUNDS[chunk + 1]
        reads[chunk].wait()

        def one(i, carry):
            f0 = lo + i * BLOCK
            v0 = vbuf[0, pl.ds(f0, BLOCK)].reshape(BLOCK * ANT, CHANNELS)
            v1 = vbuf[1, pl.ds(f0, BLOCK)].reshape(BLOCK * ANT, CHANNELS)
            g = jnp.dot(v0, table[0], preferred_element_type=jnp.float32)
            g = g + jnp.dot(v1, table[1], preferred_element_type=jnp.float32)
            gbuf[pl.ds(pl.multiple_of(f0 * ANT, 8), BLOCK * ANT)] = g
            return carry

        lax.fori_loop(0, (up - lo + BLOCK - 1) // BLOCK, one, 0)

        s0 = chunk * WIDTH * ANT
        size = WIDTH * ANT
        pair = gbuf[pl.ds(s0, size + ANT), 0:128] + gbuf[pl.ds(s0 + 2 * ANT, size + ANT), 128:256]
        total = pair[:size] + pltpu.roll(pair[ANT:], 64, 1)
        cbuf[...] = total
        for a in range(ANT):
            one_ant = cbuf[pl.ds(a, WIDTH, stride=ANT), :]
            turned = one_ant.T[0 : 2 * BAND]
            tbuf[pl.ds(a, 2 * BAND, stride=ANT), :] = turned
        kept = flags[:, pl.ds(chunk * WIDTH, WIDTH)].astype(jnp.float32)
        spectra = tbuf[...].reshape(2, GROUPS, PER, ANT, WIDTH) * kept[None, None, None]
        sbuf[chunk] = spectra.astype(jnp.bfloat16)

    def turn(chunk):
        def send(d, carry):
            j = (k + d) % GROUPS
            pltpu.make_async_remote_copy(
                src_ref=sbuf.at[chunk, :, j],
                dst_ref=rows.at[c, chunk, :, :, k],
                send_sem=turn_send.at[chunk],
                recv_sem=turn_recv.at[chunk],
                device_id=(j, r, c),
                device_id_type=MESH,
            ).start()
            return carry

        lax.fori_loop(1, GROUPS, send, 0)
        pltpu.make_async_copy(sbuf.at[chunk, :, k], rows.at[c, chunk, :, :, k], turn_recv.at[chunk]).start()

    def turned(chunk):
        whole = rows.at[c, chunk]
        pltpu.make_async_copy(whole, whole, turn_recv.at[chunk]).wait()

    def swap(chunk, slot, index):
        copy = pltpu.make_async_remote_copy(
            src_ref=rows.at[slot, chunk],
            dst_ref=rows.at[slot, chunk],
            send_sem=swap_send.at[chunk, index],
            recv_sem=row_recv.at[chunk, slot],
            device_id=mate,
            device_id_type=MESH,
        )
        copy.start()
        return copy

    def line_copy(p, index):
        chunk, source, offset, crosses = PLAN[p][index]
        src = rows.at[c, chunk] if source == p else cols.at[source, chunk]
        dst = rows.at[c, chunk] if crosses else cols.at[source, chunk]
        sem = row_recv.at[chunk, c] if crosses else col_recv.at[chunk, source]
        return pltpu.make_async_remote_copy(
            src_ref=src, dst_ref=dst, send_sem=line_send.at[index], recv_sem=sem,
            device_id=at_plane(offset), device_id_type=MESH,
        )

    def wait_col(chunk, source):
        piece = cols.at[source, chunk]
        pltpu.make_async_copy(piece, piece, col_recv.at[chunk, source]).wait()

    def wait_row(chunk, slot):
        piece = rows.at[slot, chunk]
        pltpu.make_async_copy(piece, piece, row_recv.at[chunk, slot]).wait()

    far = (1 - hi) * 2 + core

    def line(p, chunk):
        got = set()
        for index, (step, source, _, _) in enumerate(PLAN[p]):
            if step != chunk:
                continue
            if source != p and source not in got:
                wait_col(chunk, source)
                got.add(source)
            line_copy(p, index).start()
        for source in range(N_ROW):
            if source != p and source not in got:
                wait_col(chunk, source)

    channelise(0)
    pl.semaphore_wait(barrier, GROUPS - 1 + 5)
    turn(0)
    channelise(1)
    turn(1)
    swaps, owns = [], []
    for chunk in range(CHUNKS):
        turned(chunk)
        for p in range(N_ROW):
            @pl.when(r == p)
            def _(p=p, chunk=chunk):
                line(p, chunk)

        own = pltpu.make_async_copy(rows.at[c, chunk], cols.at[r, chunk], own_sem.at[chunk])
        own.start()
        owns.append(own)
        swaps.append(swap(chunk, c, 0))
        wait_row(chunk, far)
        swaps.append(swap(chunk, far, 1))
    for chunk in range(CHUNKS):
        wait_row(chunk, hi * 2 + other)
        wait_row(chunk, (1 - hi) * 2 + other)
    for copy in owns:
        copy.wait()
    for copy in swaps:
        copy.wait_send()
    for chunk in range(CHUNKS):
        sent = sbuf.at[chunk, :, pl.ds(0, GROUPS - 1)]
        pltpu.make_async_copy(sent, sent, turn_send.at[chunk]).wait()
    for p in range(N_ROW):
        @pl.when(r == p)
        def _(p=p):
            for index in range(len(PLAN[p])):
                line_copy(p, index).wait_send()


def gather(volt, table, flags):
    shape = jax.ShapeDtypeStruct((N_ROW, CHUNKS, 2, PER, GROUPS, ANT, WIDTH), jnp.bfloat16)
    anywhere = pl.BlockSpec(memory_space=pl.ANY)
    inside = pl.BlockSpec(memory_space=pltpu.VMEM)
    most = max(len(plan) for plan in PLAN.values())
    return pl.pallas_call(
        gather_kernel,
        out_shape=(shape, shape),
        in_specs=[anywhere, inside, inside],
        out_specs=(anywhere, anywhere),
        scratch_shapes=[
            pltpu.VMEM((2, PADDED, ANT, CHANNELS), jnp.bfloat16),
            pltpu.VMEM((PADDED * ANT, 256), jnp.float32),
            pltpu.VMEM((WIDTH * ANT, 128), jnp.float32),
            pltpu.VMEM((2 * BAND * ANT, WIDTH), jnp.float32),
            pltpu.VMEM((CHUNKS, 2, GROUPS, PER, ANT, WIDTH), jnp.bfloat16),
            pltpu.SemaphoreType.DMA((CHUNKS,)),
            pltpu.SemaphoreType.DMA((CHUNKS,)),
            pltpu.SemaphoreType.DMA((CHUNKS,)),
            pltpu.SemaphoreType.DMA((CHUNKS,)),
            pltpu.SemaphoreType.DMA((most,)),
            pltpu.SemaphoreType.DMA((CHUNKS, N_ROW)),
            pltpu.SemaphoreType.DMA((CHUNKS, N_ROW)),
            pltpu.SemaphoreType.DMA((CHUNKS, 2)),
        ],
        compiler_params=pltpu.CompilerParams(
            collective_id=0, has_side_effects=True, vmem_limit_bytes=56 * 1024 * 1024
        ),
        name="gather",
    )(volt, table, flags)


def power_kernel(rows, cols, out):
    def laid(ref, q):
        return [ref[:, chunk, q, 0].reshape(N_ROW * GROUPS * ANT, WIDTH) for chunk in range(CHUNKS)]

    re, im = laid(rows, 0), laid(rows, 1)
    first = jnp.concatenate(re + im, axis=1)
    second = jnp.concatenate(im + [-x for x in re], axis=1)
    column = jnp.concatenate(laid(cols, 0) + laid(cols, 1), axis=1)
    for part, left in enumerate((first, second)):
        power = lax.dot_general(left, column, (((1,), (1,)), ((), ())), preferred_element_type=jnp.float32)
        power = power * (1.0 / math.sqrt(SPECTRA))
        for g in range(N_ROW):
            out[part, 0, pl.ds(g, 512, stride=N_ROW), :] = power[:, g * 128 : (g + 1) * 128]


def power(rows, cols):
    spec = pl.BlockSpec((N_ROW, CHUNKS, 2, 1, GROUPS, ANT, WIDTH), lambda j: (0, 0, 0, j, 0, 0, 0))
    return pl.pallas_call(
        power_kernel,
        out_shape=jax.ShapeDtypeStruct((2, PER, 512 * N_ROW, 128), jnp.float32),
        grid=(PER,),
        in_specs=[spec, spec],
        out_specs=pl.BlockSpec((2, 1, 512 * N_ROW, 128), lambda j: (0, j, 0, 0)),
        compiler_params=pltpu.CompilerParams(vmem_limit_bytes=48 * 1024 * 1024),
        name="power",
    )(rows, cols)


def on_device(voltages, fir_window, flags):
    frames = voltages.reshape(2, ANT, FRAMES, CHANNELS).transpose(0, 2, 1, 3)
    weight = (fir_window / math.sqrt(TAPS * CHANNELS)).T
    table = weight[None, :, :, None] * jnp.asarray(basis())[:, :, None, :]
    table = table.astype(jnp.bfloat16).reshape(2, CHANNELS, TAPS * 2 * BAND)
    rows, cols = gather(frames, table, flags)
    return power(rows, cols).reshape(2, PER, 512, N_ROW, 128)


def solution(mesh):
    return jax.shard_map(
        on_device,
        mesh=mesh,
        in_specs=(P(None, ("row", "col", "chan"), None), P(), P(("row", "col", "chan"), None)),
        out_specs=P(None, "chan", "row", None, "col"),
        check_vma=False,
    )
```

```python
import math

import jax
import jax.numpy as jnp
import numpy as np
from jax import lax
from jax.experimental import pallas as pl
from jax.experimental.pallas import tpu as pltpu
from jax.sharding import PartitionSpec as P

MESH = pl.DeviceIdType.MESH

CHANNELS = 1024
TAPS = 4
BAND = 32
SPECTRA = 256
FRAMES = SPECTRA + TAPS - 1
ANT = 8
GROUPS = 16
PER = BAND // GROUPS
N_ROW = 4
PLANES = 8
CHUNKS = 4
WIDTH = SPECTRA // CHUNKS
BOUNDS = (0, 68, 132, 196, FRAMES)
PADDED = 260

PLAN = {
    0: [(0, 1, False), (2, -2, True), (3, -1, True)],
    1: [(1, 1, False), (1, -1, False), (0, 1, False), (2, -1, False), (3, -1, False)],
    2: [(2, -1, False), (2, 1, False), (3, -1, False), (1, 1, False), (0, 1, False)],
    3: [(3, -1, False), (1, 2, True), (0, 1, True)],
}
MOST = 5
LATE = {1: 1, 2: 1}
EARLY = 2
LAG = 2


def steps(p):
    todo = []
    for now in range(CHUNKS + N_ROW - 1):
        step = []
        if now < CHUNKS:
            for index, (source, _, _) in enumerate(PLAN[p]):
                if source == p and (LATE.get(p) != index or now < EARLY):
                    step.append((now, index))
        behind = []
        for index, (source, _, _) in enumerate(PLAN[p]):
            chunk = now - abs(source - p)
            if source != p and 0 <= chunk < CHUNKS:
                behind.append((chunk, index))
        todo.append(step + sorted(behind, key=lambda item: -item[0]))
    if p in LATE:
        todo.append([(chunk, LATE[p]) for chunk in range(EARLY, CHUNKS)])
    return todo[:CHUNKS] + [sum(todo[CHUNKS:], [])]


def basis():
    n = np.arange(CHANNELS)[:, None]
    k = np.arange(BAND)[None, :]
    angle = ((n * k) % CHANNELS).astype(np.float32) * np.float32(2.0 * math.pi / CHANNELS)
    cos, sin = np.cos(angle), np.sin(angle)
    return np.stack([np.concatenate([cos, -sin] * 2, 1), np.concatenate([sin, cos] * 2, 1)])


def gather_kernel(
    volt, waves, window, flags, rows, cols,
    vbuf, wbuf, fbuf, kbuf, table, gbuf, cbuf, tbuf, sbuf,
    volt_sem, small_sem, turn_send, turn_recv, own_sem, line_send, row_recv, col_recv, swap_send,
):
    k = lax.axis_index("chan")
    r = lax.axis_index("row")
    c = lax.axis_index("col")
    hi, core = c // 2, c % 2
    plane = hi * N_ROW + r
    other = 1 - core

    def at_plane(offset):
        z = (plane + offset + PLANES) % PLANES
        return (k, z % N_ROW, (z // N_ROW) * 2 + core)

    mate = (k, r, hi * 2 + other)

    small = [
        pltpu.make_async_copy(window, fbuf, small_sem.at[0]),
        pltpu.make_async_copy(waves, wbuf, small_sem.at[1]),
        pltpu.make_async_copy(flags, kbuf, small_sem.at[2]),
    ]
    reads = []
    for chunk in range(CHUNKS):
        lo, up = BOUNDS[chunk], BOUNDS[chunk + 1]
        reads.append(pltpu.make_async_copy(
            volt.at[:, pl.ds(lo, up - lo)], vbuf.at[:, pl.ds(lo, up - lo)], volt_sem.at[chunk]
        ))
    small[0].start()
    small[1].start()
    reads[0].start()
    small[2].start()
    for copy in reads[1:]:
        copy.start()

    barrier = pltpu.get_barrier_semaphore()

    def greet(d, carry):
        pl.semaphore_signal(barrier, inc=1, device_id=((k + d) % GROUPS, r, c), device_id_type=MESH)
        return carry

    lax.fori_loop(1, GROUPS, greet, 0)
    for offset in (-2, -1, 1, 2):
        pl.semaphore_signal(barrier, inc=1, device_id=at_plane(offset), device_id_type=MESH)
    pl.semaphore_signal(barrier, inc=1, device_id=mate, device_id_type=MESH)

    small[0].wait()
    weight = fbuf[...] * (1.0 / math.sqrt(TAPS * CHANNELS))
    weight = jnp.concatenate([weight, weight], axis=0).T
    small[1].wait()
    lane = lax.broadcasted_iota(jnp.int32, (CHANNELS, 128), 1)
    for half in range(2):
        scale = jnp.where(lane < 64, weight[:, 2 * half : 2 * half + 1], weight[:, 2 * half + 1 : 2 * half + 2])
        for part in range(2):
            table[part, :, half * 128 : (half + 1) * 128] = (wbuf[part] * scale).astype(jnp.bfloat16)

    def channelise(chunk):
        lo, up = BOUNDS[chunk], BOUNDS[chunk + 1]
        reads[chunk].wait()
        block = (min(up + 1, PADDED) - lo) // 2
        for f0 in (lo, lo + block):
            v0 = vbuf[0, f0 : f0 + block].reshape(block * ANT, CHANNELS)
            v1 = vbuf[1, f0 : f0 + block].reshape(block * ANT, CHANNELS)
            g = jnp.dot(v0, table[0], preferred_element_type=jnp.float32)
            g = g + jnp.dot(v1, table[1], preferred_element_type=jnp.float32)
            gbuf[f0 * ANT : (f0 + block) * ANT] = g

        s0 = chunk * WIDTH * ANT
        size = WIDTH * ANT
        pair = gbuf[pl.ds(s0, size + ANT), 0:128] + gbuf[pl.ds(s0 + 2 * ANT, size + ANT), 128:256]
        cbuf[...] = pair[:size] + pltpu.roll(pair[ANT:], 64, 1)
        for a in range(ANT):
            turned = cbuf[pl.ds(a, WIDTH, stride=ANT), :].T
            both = jnp.concatenate([turned[0:BAND], turned[BAND : 2 * BAND]], axis=1)
            tbuf[pl.ds(a, BAND, stride=ANT), :] = both
        if chunk == 0:
            small[2].wait()
        kept = kbuf[:, chunk * WIDTH : (chunk + 1) * WIDTH].astype(jnp.float32)
        kept = jnp.concatenate([kept, kept], axis=1)
        spectra = tbuf[...].reshape(GROUPS, PER, ANT, 2 * WIDTH) * kept[None, None]
        sbuf[chunk] = spectra.astype(jnp.bfloat16)

    def turn(chunk):
        def send(d, carry):
            j = (k + d) % GROUPS
            pltpu.make_async_remote_copy(
                src_ref=sbuf.at[chunk, j],
                dst_ref=rows.at[c, chunk, :, k],
                send_sem=turn_send.at[chunk],
                recv_sem=turn_recv.at[chunk],
                device_id=(j, r, c),
                device_id_type=MESH,
            ).start()
            return carry

        lax.fori_loop(1, GROUPS, send, 0)
        pltpu.make_async_copy(sbuf.at[chunk, k], rows.at[c, chunk, :, k], turn_recv.at[chunk]).start()

    def turned(chunk):
        whole = rows.at[c, chunk]
        pltpu.make_async_copy(whole, whole, turn_recv.at[chunk]).wait()

    def swap(chunk, slot, index):
        copy = pltpu.make_async_remote_copy(
            src_ref=rows.at[slot, chunk],
            dst_ref=rows.at[slot, chunk],
            send_sem=swap_send.at[chunk, index],
            recv_sem=row_recv.at[chunk, slot],
            device_id=mate,
            device_id_type=MESH,
        )
        copy.start()
        return copy

    def line_copy(p, chunk, index):
        source, offset, crosses = PLAN[p][index]
        src = rows.at[c, chunk] if source == p else cols.at[source, chunk]
        dst = rows.at[c, chunk] if crosses else cols.at[source, chunk]
        sem = row_recv.at[chunk, c] if crosses else col_recv.at[chunk, source]
        return pltpu.make_async_remote_copy(
            src_ref=src, dst_ref=dst, send_sem=line_send.at[chunk, index], recv_sem=sem,
            device_id=at_plane(offset), device_id_type=MESH,
        )

    def wait_col(chunk, source):
        piece = cols.at[source, chunk]
        pltpu.make_async_copy(piece, piece, col_recv.at[chunk, source]).wait()

    def wait_row(chunk, slot):
        piece = rows.at[slot, chunk]
        pltpu.make_async_copy(piece, piece, row_recv.at[chunk, slot]).wait()

    far = (1 - hi) * 2 + core

    def each_place(act):
        for p in range(N_ROW):
            @pl.when(r == p)
            def _(p=p):
                act(p)

    def send_step(p, step):
        for chunk, index in steps(p)[step]:
            source = PLAN[p][index][0]
            if source != p:
                wait_col(chunk, source)
            line_copy(p, chunk, index).start()
        if step == CHUNKS:
            relayed = [source for source, _, _ in PLAN[p]]
            for source in range(N_ROW):
                if source not in relayed:
                    for chunk in range(CHUNKS):
                        wait_col(chunk, source)

    swaps, owns = [], []

    def sends(chunk):
        turned(chunk)
        each_place(lambda p: send_step(p, chunk))
        own = pltpu.make_async_copy(rows.at[c, chunk], cols.at[r, chunk], own_sem.at[chunk])
        own.start()
        owns.append(own)
        swaps.append(swap(chunk, c, 0))

    for chunk in range(CHUNKS):
        channelise(chunk)
        if chunk == 0:
            pl.semaphore_wait(barrier, GROUPS - 1 + 5)
        turn(chunk)
        if chunk >= LAG:
            sends(chunk - LAG)
    for chunk in range(CHUNKS - LAG, CHUNKS):
        sends(chunk)
    each_place(lambda p: send_step(p, CHUNKS))
    for chunk in range(CHUNKS):
        wait_row(chunk, far)
        swaps.append(swap(chunk, far, 1))
    for copy in owns:
        copy.wait()
    for chunk in range(CHUNKS):
        sent = sbuf.at[chunk, pl.ds(0, GROUPS - 1)]
        pltpu.make_async_copy(sent, sent, turn_send.at[chunk]).wait()
    for copy in swaps:
        copy.wait_send()

    def finish(p):
        for chunk in range(CHUNKS):
            for index in range(len(PLAN[p])):
                line_copy(p, chunk, index).wait_send()

    each_place(finish)
    for chunk in range(CHUNKS):
        wait_row(chunk, hi * 2 + other)
        wait_row(chunk, (1 - hi) * 2 + other)


def gather(volt, window, flags):
    shape = jax.ShapeDtypeStruct((N_ROW, CHUNKS, PER, GROUPS, ANT, 2 * WIDTH), jnp.bfloat16)
    anywhere = pl.BlockSpec(memory_space=pltpu.HBM)
    inside = pl.BlockSpec(memory_space=pltpu.VMEM)
    return pl.pallas_call(
        gather_kernel,
        out_shape=(shape, shape),
        in_specs=[anywhere] * 4,
        out_specs=(inside, inside),
        scratch_shapes=[
            pltpu.VMEM((2, PADDED, ANT, CHANNELS), jnp.bfloat16),
            pltpu.VMEM((2, CHANNELS, 128), jnp.float32),
            pltpu.VMEM((TAPS, CHANNELS), jnp.float32),
            pltpu.VMEM((ANT, SPECTRA), jnp.int32),
            pltpu.VMEM((2, CHANNELS, 256), jnp.bfloat16),
            pltpu.VMEM((PADDED * ANT, 256), jnp.float32),
            pltpu.VMEM((WIDTH * ANT, 128), jnp.float32),
            pltpu.VMEM((BAND * ANT, 2 * WIDTH), jnp.float32),
            pltpu.VMEM((CHUNKS, GROUPS, PER, ANT, 2 * WIDTH), jnp.bfloat16),
            pltpu.SemaphoreType.DMA((CHUNKS,)),
            pltpu.SemaphoreType.DMA((3,)),
            pltpu.SemaphoreType.DMA((CHUNKS,)),
            pltpu.SemaphoreType.DMA((CHUNKS,)),
            pltpu.SemaphoreType.DMA((CHUNKS,)),
            pltpu.SemaphoreType.DMA((CHUNKS, MOST)),
            pltpu.SemaphoreType.DMA((CHUNKS, N_ROW)),
            pltpu.SemaphoreType.DMA((CHUNKS, N_ROW)),
            pltpu.SemaphoreType.DMA((CHUNKS, 2)),
        ],
        compiler_params=pltpu.CompilerParams(
            collective_id=0, has_side_effects=True, vmem_limit_bytes=40 * 1024 * 1024
        ),
        name="gather",
    )(*(pltpu.with_memory_space_constraint(x, pltpu.HBM) for x in (volt, jnp.asarray(basis()), window, flags)))


def power_kernel(rows, cols, out):
    ch = pl.program_id(0)
    half = pl.program_id(1)
    side = N_ROW // 2
    here = [rows[pl.ds(half * side, side), t, ch].reshape(side * GROUPS * ANT, 2 * WIDTH) for t in range(CHUNKS)]
    turned = [jnp.concatenate([x[:, WIDTH:], -x[:, :WIDTH]], axis=1) for x in here]
    first = jnp.concatenate(here, axis=1)
    second = jnp.concatenate(turned, axis=1)
    column = jnp.concatenate(
        [cols[:, t, ch].reshape(N_ROW * GROUPS * ANT, 2 * WIDTH) for t in range(CHUNKS)], axis=1
    )
    for part, left in enumerate((first, second)):
        power = lax.dot_general(left, column, (((1,), (1,)), ((), ())), preferred_element_type=jnp.float32)
        power = power * (1.0 / math.sqrt(SPECTRA))
        for g in range(N_ROW):
            out[part, 0, pl.ds(g, side * 128, stride=N_ROW), :] = power[:, g * 128 : (g + 1) * 128]


def power(rows, cols):
    inside = pl.BlockSpec(memory_space=pltpu.VMEM)
    return pl.pallas_call(
        power_kernel,
        out_shape=jax.ShapeDtypeStruct((2, PER, 512 * N_ROW, 128), jnp.float32),
        grid=(PER, 2),
        in_specs=[inside, inside],
        out_specs=pl.BlockSpec((2, 1, 256 * N_ROW, 128), lambda j, half: (0, j, half, 0)),
        compiler_params=pltpu.CompilerParams(vmem_limit_bytes=48 * 1024 * 1024),
        name="power",
    )(rows, cols)


def on_device(voltages, fir_window, flags):
    frames = voltages.reshape(2, ANT, FRAMES, CHANNELS).transpose(0, 2, 1, 3)
    rows, cols = gather(frames, fir_window, flags)
    return power(rows, cols).reshape(2, PER, 512, N_ROW, 128)


def solution(mesh):
    return jax.shard_map(
        on_device,
        mesh=mesh,
        in_specs=(P(None, ("row", "col", "chan"), None), P(), P(("row", "col", "chan"), None)),
        out_specs=P(None, "chan", "row", None, "col"),
        check_vma=False,
    )
```

```python
import math

import jax
import jax.numpy as jnp
import numpy as np
from jax import lax
from jax.experimental import pallas as pl
from jax.experimental.pallas import tpu as pltpu
from jax.sharding import PartitionSpec as P

MESH = pl.DeviceIdType.MESH

CHANNELS = 1024
TAPS = 4
BAND = 32
SPECTRA = 256
FRAMES = SPECTRA + TAPS - 1
ANT = 8
GROUPS = 16
PER = BAND // GROUPS
N_ROW = 4
PLANES = 8
CHUNKS = 4
WIDTH = SPECTRA // CHUNKS
BOUNDS = (0, 68, 132, 196, FRAMES)
PADDED = 260

ORDER = {
    0: [
        (0, 0, 1), (0, 1, 1), (0, 2, 1), (0, 3, 1), (2, 0, -2), (2, 1, -2), (2, 2, -2), (3, 0, -1),
        (3, 1, -1), (3, 2, -1), (3, 3, -1), (2, 3, -2),
    ],
    1: [
        (1, 0, -1), (1, 0, 1), (1, 1, -1), (1, 1, 1), (1, 2, -1), (1, 2, 1), (0, 0, 1), (2, 0, -1),
        (0, 1, 1), (2, 1, -1), (0, 2, 1), (2, 2, -1), (0, 3, 1), (3, 0, -1), (1, 3, 1), (3, 1, -1),
        (3, 2, -1), (3, 3, -1), (2, 3, -1), (1, 3, -1),
    ],
    2: [
        (2, 0, -1), (2, 0, 1), (2, 1, -1), (2, 1, 1), (2, 2, -1), (2, 2, 1), (1, 0, 1), (3, 0, -1),
        (1, 1, 1), (3, 1, -1), (1, 2, 1), (3, 2, -1), (0, 0, 1), (3, 3, -1), (0, 1, 1), (2, 3, -1),
        (0, 2, 1), (0, 3, 1), (1, 3, 1), (2, 3, 1),
    ],
    3: [
        (3, 0, -1), (3, 1, -1), (3, 2, -1), (3, 3, -1), (1, 0, 2), (1, 1, 2), (1, 2, 2), (0, 0, 1),
        (0, 1, 1), (0, 2, 1), (0, 3, 1), (1, 3, 2),
    ],
}
MOST = 20
PIECES = 4
LAG = 3


def basis():
    n = np.arange(CHANNELS)[:, None]
    k = np.arange(BAND)[None, :]
    angle = ((n * k) % CHANNELS).astype(np.float32) * np.float32(2.0 * math.pi / CHANNELS)
    cos, sin = np.cos(angle), np.sin(angle)
    return np.stack([np.concatenate([cos, -sin] * 2, 1), np.concatenate([sin, cos] * 2, 1)])


def gather_kernel(
    volt, waves, window, flags, rows, cols,
    vbuf, wbuf, fbuf, kbuf, table, gbuf, cbuf, tbuf, sbuf,
    volt_sem, small_sem, turn_send, turn_recv, own_sem, line_send, row_recv, col_recv, swap_send,
):
    k = lax.axis_index("chan")
    r = lax.axis_index("row")
    c = lax.axis_index("col")
    hi, core = c // 2, c % 2
    plane = hi * N_ROW + r
    other = 1 - core

    def at_plane(offset):
        z = (plane + offset + PLANES) % PLANES
        return (k, z % N_ROW, (z // N_ROW) * 2 + core)

    mate = (k, r, hi * 2 + other)

    small = [
        pltpu.make_async_copy(window, fbuf, small_sem.at[0]),
        pltpu.make_async_copy(waves, wbuf, small_sem.at[1]),
        pltpu.make_async_copy(flags, kbuf, small_sem.at[2]),
    ]
    reads = []
    for chunk in range(CHUNKS):
        lo, up = BOUNDS[chunk], BOUNDS[chunk + 1]
        reads.append(pltpu.make_async_copy(
            volt.at[:, pl.ds(lo, up - lo)], vbuf.at[:, pl.ds(lo, up - lo)], volt_sem.at[chunk]
        ))
    small[0].start()
    small[1].start()
    reads[0].start()
    small[2].start()

    barrier = pltpu.get_barrier_semaphore()

    def greet(d, carry):
        pl.semaphore_signal(barrier, inc=1, device_id=((k + d) % GROUPS, r, c), device_id_type=MESH)
        return carry

    lax.fori_loop(1, GROUPS, greet, 0)
    for offset in (-2, -1, 1, 2):
        pl.semaphore_signal(barrier, inc=1, device_id=at_plane(offset), device_id_type=MESH)
    pl.semaphore_signal(barrier, inc=1, device_id=mate, device_id_type=MESH)

    small[0].wait()
    weight = fbuf[...] * (1.0 / math.sqrt(TAPS * CHANNELS))
    weight = jnp.concatenate([weight, weight], axis=0).T
    small[1].wait()
    lane = lax.broadcasted_iota(jnp.int32, (CHANNELS, 128), 1)
    for half in range(2):
        scale = jnp.where(lane < 64, weight[:, 2 * half : 2 * half + 1], weight[:, 2 * half + 1 : 2 * half + 2])
        for part in range(2):
            table[part, :, half * 128 : (half + 1) * 128] = (wbuf[part] * scale).astype(jnp.bfloat16)

    def channelise(chunk):
        lo, up = BOUNDS[chunk], BOUNDS[chunk + 1]
        reads[chunk].wait()
        if chunk == 0:
            for copy in reads[1:]:
                copy.start()
        block = (min(up + 1, PADDED) - lo) // 2
        for f0 in (lo, lo + block):
            v0 = vbuf[0, f0 : f0 + block].reshape(block * ANT, CHANNELS)
            v1 = vbuf[1, f0 : f0 + block].reshape(block * ANT, CHANNELS)
            g = jnp.dot(v0, table[0], preferred_element_type=jnp.float32)
            g = g + jnp.dot(v1, table[1], preferred_element_type=jnp.float32)
            gbuf[f0 * ANT : (f0 + block) * ANT] = g

        s0 = chunk * WIDTH * ANT
        size = WIDTH * ANT
        pair = gbuf[pl.ds(s0, size + ANT), 0:128] + gbuf[pl.ds(s0 + 2 * ANT, size + ANT), 128:256]
        cbuf[...] = pair[:size] + pltpu.roll(pair[ANT:], 64, 1)
        for a in range(ANT):
            turned = cbuf[pl.ds(a, WIDTH, stride=ANT), :].T
            both = jnp.concatenate([turned[0:BAND], turned[BAND : 2 * BAND]], axis=1)
            tbuf[pl.ds(a, BAND, stride=ANT), :] = both
        if chunk == 0:
            small[2].wait()
        kept = kbuf[:, chunk * WIDTH : (chunk + 1) * WIDTH].astype(jnp.float32)
        kept = jnp.concatenate([kept, kept], axis=1)
        spectra = tbuf[...].reshape(GROUPS, PER, ANT, 2 * WIDTH) * kept[None, None]
        sbuf[chunk] = spectra.astype(jnp.bfloat16)

    def turn(chunk):
        def send(d, carry):
            j = (k + d) % GROUPS
            pltpu.make_async_remote_copy(
                src_ref=sbuf.at[chunk, j],
                dst_ref=rows.at[c, chunk, :, k],
                send_sem=turn_send.at[chunk],
                recv_sem=turn_recv.at[chunk],
                device_id=(j, r, c),
                device_id_type=MESH,
            ).start()
            return carry

        lax.fori_loop(1, GROUPS, send, 0)
        pltpu.make_async_copy(sbuf.at[chunk, k], rows.at[c, chunk, :, k], turn_recv.at[chunk]).start()

    def turned(chunk):
        whole = rows.at[c, chunk]
        pltpu.make_async_copy(whole, whole, turn_recv.at[chunk]).wait()

    def swap(chunk, slot, index):
        copy = pltpu.make_async_remote_copy(
            src_ref=rows.at[slot, chunk],
            dst_ref=rows.at[slot, chunk],
            send_sem=swap_send.at[chunk, index],
            recv_sem=row_recv.at[chunk, slot],
            device_id=mate,
            device_id_type=MESH,
        )
        copy.start()
        return copy

    def line_copy(p, index):
        source, chunk, offset = ORDER[p][index]
        crosses = not 0 <= p + offset < N_ROW
        src = rows.at[c, chunk] if source == p else cols.at[source, chunk]
        dst = rows.at[c, chunk] if crosses else cols.at[source, chunk]
        sem = row_recv.at[chunk, c] if crosses else col_recv.at[chunk, source]
        return pltpu.make_async_remote_copy(
            src_ref=src, dst_ref=dst, send_sem=line_send.at[index], recv_sem=sem,
            device_id=at_plane(offset), device_id_type=MESH,
        )

    def wait_col(chunk, source):
        piece = cols.at[source, chunk]
        pltpu.make_async_copy(piece, piece, col_recv.at[chunk, source]).wait()

    def wait_row(chunk, slot):
        piece = rows.at[slot, chunk]
        pltpu.make_async_copy(piece, piece, row_recv.at[chunk, slot]).wait()

    far = (1 - hi) * 2 + core

    def each_place(act):
        for p in range(N_ROW):
            @pl.when(r == p)
            def _(p=p):
                act(p)

    def first_need(p, chunk):
        for index, (source, step, _) in enumerate(ORDER[p]):
            if (source == p and step >= chunk) or (source != p and chunk < CHUNKS):
                return index
        return len(ORDER[p])

    def send_step(p, chunk):
        for index in range(first_need(p, chunk), first_need(p, chunk + 1)):
            source, step, _ = ORDER[p][index]
            if source != p and all(item[:2] != (source, step) for item in ORDER[p][:index]):
                wait_col(step, source)
            line_copy(p, index).start()
        if chunk == CHUNKS - 1:
            relayed = [item[:2] for item in ORDER[p]]
            for source in range(N_ROW):
                for step in range(CHUNKS):
                    if source != p and (source, step) not in relayed:
                        wait_col(step, source)

    swaps, owns = [], []

    def sends(chunk):
        turned(chunk)
        swaps.append(swap(chunk, c, 0))
        own = pltpu.make_async_copy(rows.at[c, chunk], cols.at[r, chunk], own_sem.at[chunk])
        own.start()
        owns.append(own)
        each_place(lambda p: send_step(p, chunk))

    for chunk in range(CHUNKS):
        channelise(chunk)
        if chunk == 0:
            pl.semaphore_wait(barrier, GROUPS - 1 + 5)
        turn(chunk)
        if chunk >= LAG:
            sends(chunk - LAG)
    for chunk in range(CHUNKS - LAG, CHUNKS):
        sends(chunk)
    for chunk in range(CHUNKS):
        wait_row(chunk, far)
        swaps.append(swap(chunk, far, 1))
    for copy in owns:
        copy.wait()
    for chunk in range(CHUNKS):
        sent = sbuf.at[chunk, pl.ds(0, GROUPS - 1)]
        pltpu.make_async_copy(sent, sent, turn_send.at[chunk]).wait()
    for copy in swaps:
        copy.wait_send()

    def finish(p):
        for index in range(len(ORDER[p])):
            line_copy(p, index).wait_send()

    each_place(finish)
    for chunk in range(CHUNKS):
        wait_row(chunk, hi * 2 + other)
        wait_row(chunk, (1 - hi) * 2 + other)


def gather(volt, window, flags):
    shape = jax.ShapeDtypeStruct((N_ROW, CHUNKS, PER, GROUPS, ANT, 2 * WIDTH), jnp.bfloat16)
    anywhere = pl.BlockSpec(memory_space=pltpu.HBM)
    inside = pl.BlockSpec(memory_space=pltpu.VMEM)
    return pl.pallas_call(
        gather_kernel,
        out_shape=(shape, shape),
        in_specs=[anywhere] * 4,
        out_specs=(inside, inside),
        scratch_shapes=[
            pltpu.VMEM((2, PADDED, ANT, CHANNELS), jnp.bfloat16),
            pltpu.VMEM((2, CHANNELS, 128), jnp.float32),
            pltpu.VMEM((TAPS, CHANNELS), jnp.float32),
            pltpu.VMEM((ANT, SPECTRA), jnp.int32),
            pltpu.VMEM((2, CHANNELS, 256), jnp.bfloat16),
            pltpu.VMEM((PADDED * ANT, 256), jnp.float32),
            pltpu.VMEM((WIDTH * ANT, 128), jnp.float32),
            pltpu.VMEM((BAND * ANT, 2 * WIDTH), jnp.float32),
            pltpu.VMEM((CHUNKS, GROUPS, PER, ANT, 2 * WIDTH), jnp.bfloat16),
            pltpu.SemaphoreType.DMA((CHUNKS,)),
            pltpu.SemaphoreType.DMA((3,)),
            pltpu.SemaphoreType.DMA((CHUNKS,)),
            pltpu.SemaphoreType.DMA((CHUNKS,)),
            pltpu.SemaphoreType.DMA((CHUNKS,)),
            pltpu.SemaphoreType.DMA((MOST,)),
            pltpu.SemaphoreType.DMA((CHUNKS, N_ROW)),
            pltpu.SemaphoreType.DMA((CHUNKS, N_ROW)),
            pltpu.SemaphoreType.DMA((CHUNKS, 2)),
        ],
        compiler_params=pltpu.CompilerParams(
            collective_id=0, has_side_effects=True, vmem_limit_bytes=40 * 1024 * 1024
        ),
        name="gather",
    )(*(pltpu.with_memory_space_constraint(x, pltpu.HBM) for x in (volt, jnp.asarray(basis()), window, flags)))


def power_kernel(rows, cols, out, held, sem):
    side = 512 // PIECES
    copies = []
    for ch in range(PER):
        row, col = (
            [ref[:, t, ch].reshape(N_ROW * GROUPS * ANT, 2 * WIDTH) for t in range(CHUNKS)] for ref in (rows, cols)
        )
        column = jnp.concatenate(col, axis=1)
        for piece in range(PIECES):
            here = [x[piece * side : (piece + 1) * side] for x in row]
            turned = [jnp.concatenate([x[:, WIDTH:], -x[:, :WIDTH]], axis=1) for x in here]
            left = jnp.concatenate([jnp.concatenate(here, axis=1), jnp.concatenate(turned, axis=1)], axis=0)
            power = lax.dot_general(left, column, (((1,), (1,)), ((), ())), preferred_element_type=jnp.float32)
            power = power * (1.0 / math.sqrt(SPECTRA))
            for part in range(2):
                for g in range(N_ROW):
                    block = power[part * side : (part + 1) * side, g * 128 : (g + 1) * 128]
                    held[ch, piece, part, pl.ds(g, side, stride=N_ROW), :] = block
            lines = pl.ds(piece * side * N_ROW, side * N_ROW)
            copy = pltpu.make_async_copy(held.at[ch, piece], out.at[:, ch, lines], sem.at[ch, piece])
            copy.start()
            copies.append(copy)
    for copy in copies:
        copy.wait()


def power(rows, cols):
    inside = pl.BlockSpec(memory_space=pltpu.VMEM)
    return pl.pallas_call(
        power_kernel,
        out_shape=jax.ShapeDtypeStruct((2, PER, 512 * N_ROW, 128), jnp.float32),
        in_specs=[inside, inside],
        out_specs=pl.BlockSpec(memory_space=pltpu.HBM),
        scratch_shapes=[
            pltpu.VMEM((PER, PIECES, 2, 512 * N_ROW // PIECES, 128), jnp.float32),
            pltpu.SemaphoreType.DMA((PER, PIECES)),
        ],
        compiler_params=pltpu.CompilerParams(vmem_limit_bytes=40 * 1024 * 1024),
        name="power",
    )(rows, cols)


def on_device(voltages, fir_window, flags):
    frames = voltages.reshape(2, ANT, FRAMES, CHANNELS).transpose(0, 2, 1, 3)
    rows, cols = gather(frames, fir_window, flags)
    return power(rows, cols).reshape(2, PER, 512, N_ROW, 128)


def solution(mesh):
    return jax.shard_map(
        on_device,
        mesh=mesh,
        in_specs=(P(None, ("row", "col", "chan"), None), P(), P(("row", "col", "chan"), None)),
        out_specs=P(None, "chan", "row", None, "col"),
        check_vma=False,
    )
```

```python
import math

import jax
import jax.numpy as jnp
import numpy as np
from jax import lax
from jax.experimental import pallas as pl
from jax.experimental.pallas import tpu as pltpu
from jax.sharding import PartitionSpec as P

MESH = pl.DeviceIdType.MESH

CHANNELS = 1024
TAPS = 4
BAND = 32
SPECTRA = 256
FRAMES = SPECTRA + TAPS - 1
ANT = 8
GROUPS = 16
PER = BAND // GROUPS
N_ROW = 4
PLANES = 8
CHUNKS = 4
WIDTH = SPECTRA // CHUNKS
BOUNDS = (0, 68, 132, 196, FRAMES)
PADDED = 260

ORDER = {
    0: [
        (0, 0, 1), (0, 1, 1), (0, 2, 1), (0, 3, 1), (2, 0, 6), (2, 1, 6), (2, 2, 6), (3, 0, 7),
        (3, 1, 7), (3, 2, 7), (2, 3, 6), (3, 3, 7),
    ],
    1: [
        (1, 0, 0), (1, 0, 2), (1, 1, 0), (1, 1, 2), (1, 2, 0), (1, 2, 2), (0, 0, 2), (2, 0, 0),
        (0, 1, 2), (2, 1, 0), (0, 2, 2), (2, 2, 0), (1, 3, 2), (3, 0, 0), (0, 3, 2), (3, 1, 0),
        (3, 2, 0), (2, 3, 0), (3, 3, 0), (4, 3, 0), (1, 3, 0),
    ],
    2: [
        (2, 0, 1), (2, 0, 3), (2, 1, 1), (2, 1, 3), (2, 2, 1), (2, 2, 3), (1, 0, 3), (3, 0, 1),
        (1, 1, 3), (3, 1, 1), (1, 2, 3), (3, 2, 1), (0, 0, 3), (2, 3, 1), (0, 1, 3), (3, 3, 1),
        (0, 2, 3), (1, 3, 3), (0, 3, 3), (7, 3, 3), (2, 3, 3),
    ],
    3: [
        (3, 0, 2), (3, 1, 2), (3, 2, 2), (3, 3, 2), (1, 0, 5), (1, 1, 5), (1, 2, 5), (0, 0, 4),
        (0, 1, 4), (0, 2, 4), (1, 3, 5), (0, 3, 4),
    ],
    4: [
        (4, 0, 5), (4, 1, 5), (4, 2, 5), (4, 3, 1), (4, 3, 5), (6, 0, 2), (6, 1, 2), (6, 2, 2),
        (7, 0, 3), (7, 1, 3), (7, 2, 3), (6, 3, 2),
    ],
    5: [
        (5, 0, 4), (5, 0, 6), (5, 1, 4), (5, 1, 6), (5, 2, 4), (5, 2, 6), (4, 0, 6), (6, 0, 4),
        (4, 1, 6), (6, 1, 4), (4, 2, 6), (6, 2, 4), (5, 3, 6), (7, 0, 4), (4, 3, 6), (7, 1, 4),
        (7, 2, 4), (6, 3, 4), (5, 3, 4), (7, 3, 4),
    ],
    6: [
        (6, 0, 5), (6, 0, 7), (6, 1, 5), (6, 1, 7), (6, 2, 5), (6, 2, 7), (5, 0, 7), (7, 0, 5),
        (5, 1, 7), (7, 1, 5), (5, 2, 7), (7, 2, 5), (4, 0, 7), (6, 3, 5), (4, 1, 7), (7, 3, 5),
        (4, 2, 7), (5, 3, 7), (6, 3, 7), (4, 3, 7),
    ],
    7: [
        (7, 0, 6), (7, 1, 6), (7, 2, 6), (7, 3, 2), (7, 3, 6), (5, 0, 1), (5, 1, 1), (5, 2, 1),
        (4, 0, 0), (4, 1, 0), (4, 2, 0), (5, 3, 1),
    ],
}
HOPS = (3,)
CROSSING = sorted({(z, t) for z, sends in ORDER.items() for _, _, t in sends if z // N_ROW != t // N_ROW})
MOST = 21
PIECES = 4
LAG = 3


def basis():
    n = np.arange(CHANNELS)[:, None]
    k = np.arange(BAND)[None, :]
    angle = ((n * k) % CHANNELS).astype(np.float32) * np.float32(2.0 * math.pi / CHANNELS)
    cos, sin = np.cos(angle), np.sin(angle)
    return np.stack([np.concatenate([cos, -sin] * 2, 1), np.concatenate([sin, cos] * 2, 1)])


def gather_kernel(
    volt, waves, window, flags, rows, cols,
    vbuf, wbuf, fbuf, kbuf, table, gbuf, cbuf, tbuf, sbuf, hop,
    volt_sem, small_sem, turn_send, turn_recv, own_sem, line_send, row_recv, col_recv, swap_send, hop_recv, answer,
):
    k = lax.axis_index("chan")
    r = lax.axis_index("row")
    c = lax.axis_index("col")
    hi, core = c // 2, c % 2
    plane = hi * N_ROW + r
    other = 1 - core

    def at_plane(z):
        return (k, z % N_ROW, (z // N_ROW) * 2 + core)

    mate = (k, r, hi * 2 + other)

    small = [
        pltpu.make_async_copy(window, fbuf, small_sem.at[0]),
        pltpu.make_async_copy(waves, wbuf, small_sem.at[1]),
        pltpu.make_async_copy(flags, kbuf, small_sem.at[2]),
    ]
    reads = []
    for chunk in range(CHUNKS):
        lo, up = BOUNDS[chunk], BOUNDS[chunk + 1]
        reads.append(pltpu.make_async_copy(
            volt.at[:, pl.ds(lo, up - lo)], vbuf.at[:, pl.ds(lo, up - lo)], volt_sem.at[chunk]
        ))
    small[0].start()
    small[1].start()
    reads[0].start()
    small[2].start()

    barrier = pltpu.get_barrier_semaphore()

    def greet(d, carry):
        pl.semaphore_signal(barrier, inc=1, device_id=((k + d) % GROUPS, r, c), device_id_type=MESH)
        return carry

    lax.fori_loop(1, GROUPS, greet, 0)
    for offset in range(1, N_ROW):
        pl.semaphore_signal(barrier, inc=1, device_id=(k, (r + offset) % N_ROW, c), device_id_type=MESH)
    pl.semaphore_signal(barrier, inc=1, device_id=mate, device_id_type=MESH)

    small[0].wait()
    weight = fbuf[...] * (1.0 / math.sqrt(TAPS * CHANNELS))
    weight = jnp.concatenate([weight, weight], axis=0).T
    small[1].wait()
    lane = lax.broadcasted_iota(jnp.int32, (CHANNELS, 128), 1)
    for half in range(2):
        scale = jnp.where(lane < 64, weight[:, 2 * half : 2 * half + 1], weight[:, 2 * half + 1 : 2 * half + 2])
        for part in range(2):
            table[part, :, half * 128 : (half + 1) * 128] = (wbuf[part] * scale).astype(jnp.bfloat16)

    def channelise(chunk):
        lo, up = BOUNDS[chunk], BOUNDS[chunk + 1]
        reads[chunk].wait()
        if chunk == 0:
            for copy in reads[1:]:
                copy.start()
        block = (min(up + 1, PADDED) - lo) // 2
        for f0 in (lo, lo + block):
            v0 = vbuf[0, f0 : f0 + block].reshape(block * ANT, CHANNELS)
            v1 = vbuf[1, f0 : f0 + block].reshape(block * ANT, CHANNELS)
            g = jnp.dot(v0, table[0], preferred_element_type=jnp.float32)
            g = g + jnp.dot(v1, table[1], preferred_element_type=jnp.float32)
            gbuf[f0 * ANT : (f0 + block) * ANT] = g

        s0 = chunk * WIDTH * ANT
        size = WIDTH * ANT
        pair = gbuf[pl.ds(s0, size + ANT), 0:128] + gbuf[pl.ds(s0 + 2 * ANT, size + ANT), 128:256]
        cbuf[...] = pair[:size] + pltpu.roll(pair[ANT:], 64, 1)
        for a in range(ANT):
            turned = cbuf[pl.ds(a, WIDTH, stride=ANT), :].T
            both = jnp.concatenate([turned[0:BAND], turned[BAND : 2 * BAND]], axis=1)
            tbuf[pl.ds(a, BAND, stride=ANT), :] = both
        if chunk == 0:
            small[2].wait()
        kept = kbuf[:, chunk * WIDTH : (chunk + 1) * WIDTH].astype(jnp.float32)
        kept = jnp.concatenate([kept, kept], axis=1)
        spectra = tbuf[...].reshape(GROUPS, PER, ANT, 2 * WIDTH) * kept[None, None]
        sbuf[chunk] = spectra.astype(jnp.bfloat16)

    def turn(chunk):
        def send(d, carry):
            j = (k + d) % GROUPS
            pltpu.make_async_remote_copy(
                src_ref=sbuf.at[chunk, j],
                dst_ref=rows.at[c, chunk, :, k],
                send_sem=turn_send.at[chunk],
                recv_sem=turn_recv.at[chunk],
                device_id=(j, r, c),
                device_id_type=MESH,
            ).start()
            return carry

        lax.fori_loop(1, GROUPS, send, 0)
        pltpu.make_async_copy(sbuf.at[chunk, k], rows.at[c, chunk, :, k], turn_recv.at[chunk]).start()

    def turned(chunk):
        whole = rows.at[c, chunk]
        pltpu.make_async_copy(whole, whole, turn_recv.at[chunk]).wait()

    def swap(chunk, slot, index):
        copy = pltpu.make_async_remote_copy(
            src_ref=rows.at[slot, chunk],
            dst_ref=rows.at[slot, chunk],
            send_sem=swap_send.at[chunk, index],
            recv_sem=row_recv.at[chunk, slot],
            device_id=mate,
            device_id_type=MESH,
        )
        copy.start()
        return copy

    def line_copy(z, index):
        source, chunk, target = ORDER[z][index]
        line, place = source // N_ROW, source % N_ROW
        slot = line * 2 + core
        if source == z:
            src = rows.at[slot, chunk]
        elif line == z // N_ROW:
            src = cols.at[place, chunk]
        else:
            src = hop.at[HOPS.index(chunk)]
        if line == target // N_ROW:
            dst, sem = cols.at[place, chunk], col_recv.at[chunk, place]
        elif target == (source + N_ROW) % PLANES:
            dst, sem = rows.at[slot, chunk], row_recv.at[chunk, slot]
        else:
            dst, sem = hop.at[HOPS.index(chunk)], hop_recv.at[HOPS.index(chunk)]
        return pltpu.make_async_remote_copy(
            src_ref=src, dst_ref=dst, send_sem=line_send.at[index], recv_sem=sem,
            device_id=at_plane(target), device_id_type=MESH,
        )

    def wait_hop(chunk):
        piece = hop.at[HOPS.index(chunk)]
        pltpu.make_async_copy(piece, piece, hop_recv.at[HOPS.index(chunk)]).wait()

    def wait_col(chunk, source):
        piece = cols.at[source, chunk]
        pltpu.make_async_copy(piece, piece, col_recv.at[chunk, source]).wait()

    def wait_row(chunk, slot):
        piece = rows.at[slot, chunk]
        pltpu.make_async_copy(piece, piece, row_recv.at[chunk, slot]).wait()

    far = (1 - hi) * 2 + core

    def each_plane(act):
        for z in range(PLANES):
            @pl.when(plane == z)
            def _(z=z):
                act(z)

    def enter(z):
        near = GROUPS - 1 + N_ROW - 1 + 1
        partners = sorted({pair[0] + pair[1] - z for pair in CROSSING if z in pair})
        if z < N_ROW:
            pl.semaphore_wait(barrier, near)
            for partner in partners:
                pl.semaphore_signal(barrier, inc=1, device_id=at_plane(partner), device_id_type=MESH)
        else:
            pl.semaphore_wait(barrier, near + len(partners))
            for sender, target in CROSSING:
                if target == z:
                    pl.semaphore_signal(answer, inc=1, device_id=at_plane(sender), device_id_type=MESH)

    def first_need(z, chunk):
        for index, (source, step, _) in enumerate(ORDER[z]):
            if (source == z and step >= chunk) or (source != z and chunk < CHUNKS):
                return index
        return len(ORDER[z])

    def send_step(z, chunk):
        for index in range(first_need(z, chunk), first_need(z, chunk + 1)):
            source, step, _ = ORDER[z][index]
            if source != z and all(item[:2] != (source, step) for item in ORDER[z][:index]):
                if source // N_ROW == z // N_ROW:
                    wait_col(step, source % N_ROW)
                else:
                    wait_hop(step)
            crossing = [i for i, item in enumerate(ORDER[z]) if item[2] // N_ROW != z // N_ROW]
            if z < N_ROW and crossing and index == crossing[0]:
                pl.semaphore_wait(answer, len([pair for pair in CROSSING if pair[0] == z]))
            line_copy(z, index).start()
        if chunk == CHUNKS - 1:
            relayed = [item[:2] for item in ORDER[z]]
            for source in range(z // N_ROW * N_ROW, (z // N_ROW + 1) * N_ROW):
                for step in range(CHUNKS):
                    if source != z and (source, step) not in relayed:
                        wait_col(step, source % N_ROW)

    swaps, owns = [], []

    def sends(chunk):
        turned(chunk)
        swaps.append(swap(chunk, c, 0))
        own = pltpu.make_async_copy(rows.at[c, chunk], cols.at[r, chunk], own_sem.at[chunk])
        own.start()
        owns.append(own)
        each_plane(lambda z: send_step(z, chunk))

    for chunk in range(CHUNKS):
        channelise(chunk)
        if chunk == 0:
            each_plane(enter)
        turn(chunk)
        if chunk >= LAG:
            sends(chunk - LAG)
    for chunk in range(CHUNKS - LAG, CHUNKS):
        sends(chunk)
    for chunk in range(CHUNKS):
        wait_row(chunk, far)
        swaps.append(swap(chunk, far, 1))
    for copy in owns:
        copy.wait()
    for chunk in range(CHUNKS):
        sent = sbuf.at[chunk, pl.ds(0, GROUPS - 1)]
        pltpu.make_async_copy(sent, sent, turn_send.at[chunk]).wait()
    for copy in swaps:
        copy.wait_send()

    def finish(z):
        for index in range(len(ORDER[z])):
            line_copy(z, index).wait_send()

    each_plane(finish)
    for chunk in range(CHUNKS):
        wait_row(chunk, hi * 2 + other)
        wait_row(chunk, (1 - hi) * 2 + other)


def gather(volt, window, flags):
    shape = jax.ShapeDtypeStruct((N_ROW, CHUNKS, PER, GROUPS, ANT, 2 * WIDTH), jnp.bfloat16)
    anywhere = pl.BlockSpec(memory_space=pltpu.HBM)
    inside = pl.BlockSpec(memory_space=pltpu.VMEM)
    return pl.pallas_call(
        gather_kernel,
        out_shape=(shape, shape),
        in_specs=[anywhere] * 4,
        out_specs=(inside, inside),
        scratch_shapes=[
            pltpu.VMEM((2, PADDED, ANT, CHANNELS), jnp.bfloat16),
            pltpu.VMEM((2, CHANNELS, 128), jnp.float32),
            pltpu.VMEM((TAPS, CHANNELS), jnp.float32),
            pltpu.VMEM((ANT, SPECTRA), jnp.int32),
            pltpu.VMEM((2, CHANNELS, 256), jnp.bfloat16),
            pltpu.VMEM((PADDED * ANT, 256), jnp.float32),
            pltpu.VMEM((WIDTH * ANT, 128), jnp.float32),
            pltpu.VMEM((BAND * ANT, 2 * WIDTH), jnp.float32),
            pltpu.VMEM((CHUNKS, GROUPS, PER, ANT, 2 * WIDTH), jnp.bfloat16),
            pltpu.VMEM((max(1, len(HOPS)), PER, GROUPS, ANT, 2 * WIDTH), jnp.bfloat16),
            pltpu.SemaphoreType.DMA((CHUNKS,)),
            pltpu.SemaphoreType.DMA((3,)),
            pltpu.SemaphoreType.DMA((CHUNKS,)),
            pltpu.SemaphoreType.DMA((CHUNKS,)),
            pltpu.SemaphoreType.DMA((CHUNKS,)),
            pltpu.SemaphoreType.DMA((MOST,)),
            pltpu.SemaphoreType.DMA((CHUNKS, N_ROW)),
            pltpu.SemaphoreType.DMA((CHUNKS, N_ROW)),
            pltpu.SemaphoreType.DMA((CHUNKS, 2)),
            pltpu.SemaphoreType.DMA((max(1, len(HOPS)),)),
            pltpu.SemaphoreType.REGULAR,
        ],
        compiler_params=pltpu.CompilerParams(
            collective_id=0, has_side_effects=True, vmem_limit_bytes=40 * 1024 * 1024
        ),
        name="gather",
    )(*(pltpu.with_memory_space_constraint(x, pltpu.HBM) for x in (volt, jnp.asarray(basis()), window, flags)))


def power_kernel(rows, cols, out, held, sem):
    side = 512 // PIECES
    copies = []
    for ch in range(PER):
        row, col = (
            [ref[:, t, ch].reshape(N_ROW * GROUPS * ANT, 2 * WIDTH) for t in range(CHUNKS)] for ref in (rows, cols)
        )
        column = jnp.concatenate(col, axis=1)
        for piece in range(PIECES):
            here = [x[piece * side : (piece + 1) * side] for x in row]
            turned = [jnp.concatenate([x[:, WIDTH:], -x[:, :WIDTH]], axis=1) for x in here]
            left = jnp.concatenate([jnp.concatenate(here, axis=1), jnp.concatenate(turned, axis=1)], axis=0)
            power = lax.dot_general(left, column, (((1,), (1,)), ((), ())), preferred_element_type=jnp.float32)
            power = power * (1.0 / math.sqrt(SPECTRA))
            for part in range(2):
                for g in range(N_ROW):
                    block = power[part * side : (part + 1) * side, g * 128 : (g + 1) * 128]
                    held[ch, piece, part, pl.ds(g, side, stride=N_ROW), :] = block
            lines = pl.ds(piece * side * N_ROW, side * N_ROW)
            copy = pltpu.make_async_copy(held.at[ch, piece], out.at[:, ch, lines], sem.at[ch, piece])
            copy.start()
            copies.append(copy)
    for copy in copies:
        copy.wait()


def power(rows, cols):
    inside = pl.BlockSpec(memory_space=pltpu.VMEM)
    return pl.pallas_call(
        power_kernel,
        out_shape=jax.ShapeDtypeStruct((2, PER, 512 * N_ROW, 128), jnp.float32),
        in_specs=[inside, inside],
        out_specs=pl.BlockSpec(memory_space=pltpu.HBM),
        scratch_shapes=[
            pltpu.VMEM((PER, PIECES, 2, 512 * N_ROW // PIECES, 128), jnp.float32),
            pltpu.SemaphoreType.DMA((PER, PIECES)),
        ],
        compiler_params=pltpu.CompilerParams(vmem_limit_bytes=40 * 1024 * 1024),
        name="power",
    )(rows, cols)


def on_device(voltages, fir_window, flags):
    frames = voltages.reshape(2, ANT, FRAMES, CHANNELS).transpose(0, 2, 1, 3)
    rows, cols = gather(frames, fir_window, flags)
    return power(rows, cols).reshape(2, PER, 512, N_ROW, 128)


def solution(mesh):
    return jax.shard_map(
        on_device,
        mesh=mesh,
        in_specs=(P(None, ("row", "col", "chan"), None), P(), P(("row", "col", "chan"), None)),
        out_specs=P(None, "chan", "row", None, "col"),
        check_vma=False,
    )
```

```python
import math

import jax
import jax.numpy as jnp
import numpy as np
from jax import lax
from jax.experimental import pallas as pl
from jax.experimental.pallas import tpu as pltpu
from jax.sharding import PartitionSpec as P

MESH = pl.DeviceIdType.MESH

CHANNELS = 1024
TAPS = 4
BAND = 32
SPECTRA = 256
FRAMES = SPECTRA + TAPS - 1
ANT = 8
GROUPS = 16
PER = BAND // GROUPS
N_ROW = 4
PLANES = 8
CHUNKS = 4
WIDTH = SPECTRA // CHUNKS
BOUNDS = (0, 68, 132, 196, FRAMES)
PADDED = 260

ORDER = {
    0: [
        (0, 0, 1), (0, 1, 1), (0, 2, 1), (0, 3, 1), (2, 0, 6), (2, 1, 6), (2, 2, 6), (3, 0, 7),
        (3, 1, 7), (3, 2, 7), (2, 3, 6), (3, 3, 7),
    ],
    1: [
        (1, 0, 0), (1, 0, 2), (1, 1, 0), (1, 1, 2), (1, 2, 0), (1, 2, 2), (0, 0, 2), (2, 0, 0),
        (0, 1, 2), (2, 1, 0), (0, 2, 2), (2, 2, 0), (1, 3, 2), (3, 0, 0), (0, 3, 2), (3, 1, 0),
        (3, 2, 0), (2, 3, 0), (3, 3, 0), (4, 3, 0), (1, 3, 0),
    ],
    2: [
        (2, 0, 1), (2, 0, 3), (2, 1, 1), (2, 1, 3), (2, 2, 1), (2, 2, 3), (1, 0, 3), (3, 0, 1),
        (1, 1, 3), (3, 1, 1), (1, 2, 3), (3, 2, 1), (0, 0, 3), (2, 3, 1), (0, 1, 3), (3, 3, 1),
        (0, 2, 3), (1, 3, 3), (0, 3, 3), (7, 3, 3), (2, 3, 3),
    ],
    3: [
        (3, 0, 2), (3, 1, 2), (3, 2, 2), (3, 3, 2), (1, 0, 5), (1, 1, 5), (1, 2, 5), (0, 0, 4),
        (0, 1, 4), (0, 2, 4), (1, 3, 5), (0, 3, 4),
    ],
    4: [
        (4, 0, 5), (4, 1, 5), (4, 2, 5), (4, 3, 1), (4, 3, 5), (6, 0, 2), (6, 1, 2), (6, 2, 2),
        (7, 0, 3), (7, 1, 3), (7, 2, 3), (6, 3, 2),
    ],
    5: [
        (5, 0, 4), (5, 0, 6), (5, 1, 4), (5, 1, 6), (5, 2, 4), (5, 2, 6), (4, 0, 6), (6, 0, 4),
        (4, 1, 6), (6, 1, 4), (4, 2, 6), (6, 2, 4), (5, 3, 6), (7, 0, 4), (4, 3, 6), (7, 1, 4),
        (7, 2, 4), (6, 3, 4), (5, 3, 4), (7, 3, 4),
    ],
    6: [
        (6, 0, 5), (6, 0, 7), (6, 1, 5), (6, 1, 7), (6, 2, 5), (6, 2, 7), (5, 0, 7), (7, 0, 5),
        (5, 1, 7), (7, 1, 5), (5, 2, 7), (7, 2, 5), (4, 0, 7), (6, 3, 5), (4, 1, 7), (7, 3, 5),
        (4, 2, 7), (5, 3, 7), (6, 3, 7), (4, 3, 7),
    ],
    7: [
        (7, 0, 6), (7, 1, 6), (7, 2, 6), (7, 3, 2), (7, 3, 6), (5, 0, 1), (5, 1, 1), (5, 2, 1),
        (4, 0, 0), (4, 1, 0), (4, 2, 0), (5, 3, 1),
    ],
}
HOPS = (3,)
CROSSING = sorted({(z, t) for z, sends in ORDER.items() for _, _, t in sends if z // N_ROW != t // N_ROW})
MOST = 21
PIECES = 4
LAG = 3


def basis():
    n = np.arange(CHANNELS)[:, None]
    k = np.arange(BAND)[None, :]
    angle = ((n * k) % CHANNELS).astype(np.float32) * np.float32(2.0 * math.pi / CHANNELS)
    cos, sin = np.cos(angle), np.sin(angle)
    return np.stack([np.concatenate([cos, -sin] * 2, 1), np.concatenate([sin, cos] * 2, 1)])


def column_of(cols, ch):
    return jnp.concatenate(
        [cols[:, t, ch].reshape(N_ROW * GROUPS * ANT, 2 * WIDTH) for t in range(CHUNKS)], axis=1
    )


def left_of(rows, ch, slot):
    here = [rows[slot, t, ch].reshape(GROUPS * ANT, 2 * WIDTH) for t in range(CHUNKS)]
    turned = [jnp.concatenate([x[:, WIDTH:], -x[:, :WIDTH]], axis=1) for x in here]
    return jnp.concatenate([jnp.concatenate(here, axis=1), jnp.concatenate(turned, axis=1)], axis=0)


def fill(out, left, column):
    power = lax.dot_general(left, column, (((1,), (1,)), ((), ())), preferred_element_type=jnp.float32)
    power = power * (1.0 / math.sqrt(SPECTRA))
    for part in range(2):
        for g in range(N_ROW):
            out[part, pl.ds(g, 128, stride=N_ROW), :] = power[part * 128 : (part + 1) * 128, g * 128 : (g + 1) * 128]


def gather_kernel(
    volt, waves, window, flags, rows, cols, near,
    vbuf, wbuf, fbuf, kbuf, table, gbuf, cbuf, tbuf, sbuf, hop,
    volt_sem, small_sem, turn_send, turn_recv, own_sem, line_send, row_recv, col_recv, swap_send, hop_recv, answer,
):
    k = lax.axis_index("chan")
    r = lax.axis_index("row")
    c = lax.axis_index("col")
    hi, core = c // 2, c % 2
    plane = hi * N_ROW + r
    other = 1 - core

    def at_plane(z):
        return (k, z % N_ROW, (z // N_ROW) * 2 + core)

    mate = (k, r, hi * 2 + other)

    small = [
        pltpu.make_async_copy(window, fbuf, small_sem.at[0]),
        pltpu.make_async_copy(waves, wbuf, small_sem.at[1]),
        pltpu.make_async_copy(flags, kbuf, small_sem.at[2]),
    ]
    reads = []
    for chunk in range(CHUNKS):
        lo, up = BOUNDS[chunk], BOUNDS[chunk + 1]
        reads.append(pltpu.make_async_copy(
            volt.at[:, pl.ds(lo, up - lo)], vbuf.at[:, pl.ds(lo, up - lo)], volt_sem.at[chunk]
        ))
    small[0].start()
    small[1].start()
    reads[0].start()
    small[2].start()

    barrier = pltpu.get_barrier_semaphore()

    def greet(d, carry):
        pl.semaphore_signal(barrier, inc=1, device_id=((k + d) % GROUPS, r, c), device_id_type=MESH)
        return carry

    lax.fori_loop(1, GROUPS, greet, 0)
    for offset in range(1, N_ROW):
        pl.semaphore_signal(barrier, inc=1, device_id=(k, (r + offset) % N_ROW, c), device_id_type=MESH)
    pl.semaphore_signal(barrier, inc=1, device_id=mate, device_id_type=MESH)

    small[0].wait()
    weight = fbuf[...] * (1.0 / math.sqrt(TAPS * CHANNELS))
    weight = jnp.concatenate([weight, weight], axis=0).T
    small[1].wait()
    lane = lax.broadcasted_iota(jnp.int32, (CHANNELS, 128), 1)
    for half in range(2):
        scale = jnp.where(lane < 64, weight[:, 2 * half : 2 * half + 1], weight[:, 2 * half + 1 : 2 * half + 2])
        for part in range(2):
            table[part, :, half * 128 : (half + 1) * 128] = (wbuf[part] * scale).astype(jnp.bfloat16)

    def channelise(chunk):
        lo, up = BOUNDS[chunk], BOUNDS[chunk + 1]
        reads[chunk].wait()
        if chunk == 0:
            for copy in reads[1:]:
                copy.start()
        block = (min(up + 1, PADDED) - lo) // 2
        for f0 in (lo, lo + block):
            v0 = vbuf[0, f0 : f0 + block].reshape(block * ANT, CHANNELS)
            v1 = vbuf[1, f0 : f0 + block].reshape(block * ANT, CHANNELS)
            g = jnp.dot(v0, table[0], preferred_element_type=jnp.float32)
            g = g + jnp.dot(v1, table[1], preferred_element_type=jnp.float32)
            gbuf[f0 * ANT : (f0 + block) * ANT] = g

        s0 = chunk * WIDTH * ANT
        size = WIDTH * ANT
        pair = gbuf[pl.ds(s0, size + ANT), 0:128] + gbuf[pl.ds(s0 + 2 * ANT, size + ANT), 128:256]
        cbuf[...] = pair[:size] + pltpu.roll(pair[ANT:], 64, 1)
        for a in range(ANT):
            turned = cbuf[pl.ds(a, WIDTH, stride=ANT), :].T
            both = jnp.concatenate([turned[0:BAND], turned[BAND : 2 * BAND]], axis=1)
            tbuf[pl.ds(a, BAND, stride=ANT), :] = both
        if chunk == 0:
            small[2].wait()
        kept = kbuf[:, chunk * WIDTH : (chunk + 1) * WIDTH].astype(jnp.float32)
        kept = jnp.concatenate([kept, kept], axis=1)
        spectra = tbuf[...].reshape(GROUPS, PER, ANT, 2 * WIDTH) * kept[None, None]
        sbuf[chunk] = spectra.astype(jnp.bfloat16)

    def turn(chunk):
        def send(d, carry):
            j = (k + d) % GROUPS
            pltpu.make_async_remote_copy(
                src_ref=sbuf.at[chunk, j],
                dst_ref=rows.at[c, chunk, :, k],
                send_sem=turn_send.at[chunk],
                recv_sem=turn_recv.at[chunk],
                device_id=(j, r, c),
                device_id_type=MESH,
            ).start()
            return carry

        lax.fori_loop(1, GROUPS, send, 0)
        pltpu.make_async_copy(sbuf.at[chunk, k], rows.at[c, chunk, :, k], turn_recv.at[chunk]).start()

    def turned(chunk):
        whole = rows.at[c, chunk]
        pltpu.make_async_copy(whole, whole, turn_recv.at[chunk]).wait()

    def swap(chunk, slot, index):
        copy = pltpu.make_async_remote_copy(
            src_ref=rows.at[slot, chunk],
            dst_ref=rows.at[slot, chunk],
            send_sem=swap_send.at[chunk, index],
            recv_sem=row_recv.at[chunk, slot],
            device_id=mate,
            device_id_type=MESH,
        )
        copy.start()
        return copy

    def line_copy(z, index):
        source, chunk, target = ORDER[z][index]
        line, place = source // N_ROW, source % N_ROW
        slot = line * 2 + core
        if source == z:
            src = rows.at[slot, chunk]
        elif line == z // N_ROW:
            src = cols.at[place, chunk]
        else:
            src = hop.at[HOPS.index(chunk)]
        if line == target // N_ROW:
            dst, sem = cols.at[place, chunk], col_recv.at[chunk, place]
        elif target == (source + N_ROW) % PLANES:
            dst, sem = rows.at[slot, chunk], row_recv.at[chunk, slot]
        else:
            dst, sem = hop.at[HOPS.index(chunk)], hop_recv.at[HOPS.index(chunk)]
        return pltpu.make_async_remote_copy(
            src_ref=src, dst_ref=dst, send_sem=line_send.at[index], recv_sem=sem,
            device_id=at_plane(target), device_id_type=MESH,
        )

    def wait_hop(chunk):
        piece = hop.at[HOPS.index(chunk)]
        pltpu.make_async_copy(piece, piece, hop_recv.at[HOPS.index(chunk)]).wait()

    def wait_col(chunk, source):
        piece = cols.at[source, chunk]
        pltpu.make_async_copy(piece, piece, col_recv.at[chunk, source]).wait()

    def wait_row(chunk, slot):
        piece = rows.at[slot, chunk]
        pltpu.make_async_copy(piece, piece, row_recv.at[chunk, slot]).wait()

    far = (1 - hi) * 2 + core

    def each_plane(act):
        for z in range(PLANES):
            @pl.when(plane == z)
            def _(z=z):
                act(z)

    def enter(z):
        near = GROUPS - 1 + N_ROW - 1 + 1
        partners = sorted({pair[0] + pair[1] - z for pair in CROSSING if z in pair})
        if z < N_ROW:
            pl.semaphore_wait(barrier, near)
            for partner in partners:
                pl.semaphore_signal(barrier, inc=1, device_id=at_plane(partner), device_id_type=MESH)
        else:
            pl.semaphore_wait(barrier, near + len(partners))
            for sender, target in CROSSING:
                if target == z:
                    pl.semaphore_signal(answer, inc=1, device_id=at_plane(sender), device_id_type=MESH)

    def first_need(z, chunk):
        for index, (source, step, _) in enumerate(ORDER[z]):
            if (source == z and step >= chunk) or (source != z and chunk < CHUNKS):
                return index
        return len(ORDER[z])

    def send_step(z, chunk):
        for index in range(first_need(z, chunk), first_need(z, chunk + 1)):
            source, step, _ = ORDER[z][index]
            if source != z and all(item[:2] != (source, step) for item in ORDER[z][:index]):
                if source // N_ROW == z // N_ROW:
                    wait_col(step, source % N_ROW)
                else:
                    wait_hop(step)
            crossing = [i for i, item in enumerate(ORDER[z]) if item[2] // N_ROW != z // N_ROW]
            if z < N_ROW and crossing and index == crossing[0]:
                pl.semaphore_wait(answer, len([pair for pair in CROSSING if pair[0] == z]))
            line_copy(z, index).start()
        if chunk == CHUNKS - 1:
            relayed = [item[:2] for item in ORDER[z]]
            for source in range(z // N_ROW * N_ROW, (z // N_ROW + 1) * N_ROW):
                for step in range(CHUNKS):
                    if source != z and (source, step) not in relayed:
                        wait_col(step, source % N_ROW)

    swaps, owns = [], []

    def sends(chunk):
        turned(chunk)
        swaps.append(swap(chunk, c, 0))
        own = pltpu.make_async_copy(rows.at[c, chunk], cols.at[r, chunk], own_sem.at[chunk])
        own.start()
        owns.append(own)
        each_plane(lambda z: send_step(z, chunk))

    for chunk in range(CHUNKS):
        channelise(chunk)
        if chunk == 0:
            each_plane(enter)
        turn(chunk)
        if chunk >= LAG:
            sends(chunk - LAG)
    for chunk in range(CHUNKS - LAG, CHUNKS):
        sends(chunk)
    for copy in owns:
        copy.wait()
    for chunk in range(CHUNKS):
        wait_row(chunk, hi * 2 + other)
    for chunk in range(CHUNKS):
        if chunk >= CHUNKS - PER:
            ch = chunk - (CHUNKS - PER)
            column = column_of(cols, ch)
            for piece in range(PIECES // 2):
                fill(near.at[ch, piece], left_of(rows, ch, hi * 2 + piece), column)
        wait_row(chunk, far)
        swaps.append(swap(chunk, far, 1))
    for chunk in range(CHUNKS):
        sent = sbuf.at[chunk, pl.ds(0, GROUPS - 1)]
        pltpu.make_async_copy(sent, sent, turn_send.at[chunk]).wait()
    for copy in swaps:
        copy.wait_send()

    def finish(z):
        for index in range(len(ORDER[z])):
            line_copy(z, index).wait_send()

    each_plane(finish)
    for chunk in range(CHUNKS):
        wait_row(chunk, (1 - hi) * 2 + other)


def gather(volt, window, flags):
    shape = jax.ShapeDtypeStruct((N_ROW, CHUNKS, PER, GROUPS, ANT, 2 * WIDTH), jnp.bfloat16)
    anywhere = pl.BlockSpec(memory_space=pltpu.HBM)
    inside = pl.BlockSpec(memory_space=pltpu.VMEM)
    return pl.pallas_call(
        gather_kernel,
        out_shape=(shape, shape, jax.ShapeDtypeStruct((PER, PIECES // 2, 2, 128 * N_ROW, 128), jnp.float32)),
        in_specs=[anywhere] * 4,
        out_specs=(inside, inside, inside),
        scratch_shapes=[
            pltpu.VMEM((2, PADDED, ANT, CHANNELS), jnp.bfloat16),
            pltpu.VMEM((2, CHANNELS, 128), jnp.float32),
            pltpu.VMEM((TAPS, CHANNELS), jnp.float32),
            pltpu.VMEM((ANT, SPECTRA), jnp.int32),
            pltpu.VMEM((2, CHANNELS, 256), jnp.bfloat16),
            pltpu.VMEM((PADDED * ANT, 256), jnp.float32),
            pltpu.VMEM((WIDTH * ANT, 128), jnp.float32),
            pltpu.VMEM((BAND * ANT, 2 * WIDTH), jnp.float32),
            pltpu.VMEM((CHUNKS, GROUPS, PER, ANT, 2 * WIDTH), jnp.bfloat16),
            pltpu.VMEM((max(1, len(HOPS)), PER, GROUPS, ANT, 2 * WIDTH), jnp.bfloat16),
            pltpu.SemaphoreType.DMA((CHUNKS,)),
            pltpu.SemaphoreType.DMA((3,)),
            pltpu.SemaphoreType.DMA((CHUNKS,)),
            pltpu.SemaphoreType.DMA((CHUNKS,)),
            pltpu.SemaphoreType.DMA((CHUNKS,)),
            pltpu.SemaphoreType.DMA((MOST,)),
            pltpu.SemaphoreType.DMA((CHUNKS, N_ROW)),
            pltpu.SemaphoreType.DMA((CHUNKS, N_ROW)),
            pltpu.SemaphoreType.DMA((CHUNKS, 2)),
            pltpu.SemaphoreType.DMA((max(1, len(HOPS)),)),
            pltpu.SemaphoreType.REGULAR,
        ],
        compiler_params=pltpu.CompilerParams(
            collective_id=0, has_side_effects=True, vmem_limit_bytes=40 * 1024 * 1024
        ),
        name="gather",
    )(*(pltpu.with_memory_space_constraint(x, pltpu.HBM) for x in (volt, jnp.asarray(basis()), window, flags)))


def power_kernel(rows, cols, near, out, held, near_sem, sem):
    hi = lax.axis_index("col") // 2
    copies = []

    def write(src, ch, slot, where):
        lines = pl.ds(pl.multiple_of(slot * 128 * N_ROW, 128 * N_ROW), 128 * N_ROW)
        copy = pltpu.make_async_copy(src, out.at[:, ch, lines], where)
        copy.start()
        copies.append(copy)

    for ch in range(PER):
        for piece in range(PIECES // 2):
            write(near.at[ch, piece], ch, hi * 2 + piece, near_sem.at[ch, piece])
    for ch in range(PER):
        column = column_of(cols, ch)
        for piece in range(PIECES // 2):
            slot = (1 - hi) * 2 + piece
            fill(held.at[ch, piece], left_of(rows, ch, slot), column)
            write(held.at[ch, piece], ch, slot, sem.at[ch, piece])
    for copy in copies:
        copy.wait()


def power(rows, cols, near):
    inside = pl.BlockSpec(memory_space=pltpu.VMEM)
    return pl.pallas_call(
        power_kernel,
        out_shape=jax.ShapeDtypeStruct((2, PER, 512 * N_ROW, 128), jnp.float32),
        in_specs=[inside, inside, inside],
        out_specs=pl.BlockSpec(memory_space=pltpu.HBM),
        scratch_shapes=[
            pltpu.VMEM((PER, PIECES // 2, 2, 128 * N_ROW, 128), jnp.float32),
            pltpu.SemaphoreType.DMA((PER, PIECES // 2)),
            pltpu.SemaphoreType.DMA((PER, PIECES // 2)),
        ],
        compiler_params=pltpu.CompilerParams(vmem_limit_bytes=40 * 1024 * 1024),
        name="power",
    )(rows, cols, near)


def on_device(voltages, fir_window, flags):
    frames = voltages.reshape(2, ANT, FRAMES, CHANNELS).transpose(0, 2, 1, 3)
    rows, cols, near = gather(frames, fir_window, flags)
    return power(rows, cols, near).reshape(2, PER, 512, N_ROW, 128)


def solution(mesh):
    return jax.shard_map(
        on_device,
        mesh=mesh,
        in_specs=(P(None, ("row", "col", "chan"), None), P(), P(("row", "col", "chan"), None)),
        out_specs=P(None, "chan", "row", None, "col"),
        check_vma=False,
    )
```

```python
import math

import jax
import jax.numpy as jnp
import numpy as np
from jax import lax
from jax.experimental import pallas as pl
from jax.experimental.pallas import tpu as pltpu
from jax.sharding import PartitionSpec as P

MESH = pl.DeviceIdType.MESH

CHANNELS = 1024
TAPS = 4
BAND = 32
SPECTRA = 256
FRAMES = SPECTRA + TAPS - 1
ANT = 8
GROUPS = 16
PER = BAND // GROUPS
N_ROW = 4
PLANES = 8
CHUNKS = 4
WIDTH = SPECTRA // CHUNKS
BOUNDS = (0, 68, 132, 196, FRAMES)
PADDED = 260

ORDER = {
    0: [
        (0, 0, 1), (0, 1, 1), (0, 2, 1), (0, 3, 1), (2, 0, 6), (2, 1, 6), (2, 2, 6), (3, 0, 7),
        (3, 1, 7), (3, 2, 7), (2, 3, 6), (3, 3, 7),
    ],
    1: [
        (1, 0, 0), (1, 0, 2), (1, 1, 0), (1, 1, 2), (1, 2, 0), (1, 2, 2), (0, 0, 2), (2, 0, 0),
        (0, 1, 2), (2, 1, 0), (0, 2, 2), (2, 2, 0), (1, 3, 2), (3, 0, 0), (0, 3, 2), (3, 1, 0),
        (3, 2, 0), (2, 3, 0), (3, 3, 0), (4, 3, 0), (1, 3, 0),
    ],
    2: [
        (2, 0, 1), (2, 0, 3), (2, 1, 1), (2, 1, 3), (2, 2, 1), (2, 2, 3), (1, 0, 3), (3, 0, 1),
        (1, 1, 3), (3, 1, 1), (1, 2, 3), (3, 2, 1), (0, 0, 3), (2, 3, 1), (0, 1, 3), (3, 3, 1),
        (0, 2, 3), (1, 3, 3), (0, 3, 3), (7, 3, 3), (2, 3, 3),
    ],
    3: [
        (3, 0, 2), (3, 1, 2), (3, 2, 2), (3, 3, 2), (1, 0, 5), (1, 1, 5), (1, 2, 5), (0, 0, 4),
        (0, 1, 4), (0, 2, 4), (1, 3, 5), (0, 3, 4),
    ],
    4: [
        (4, 0, 5), (4, 1, 5), (4, 2, 5), (4, 3, 1), (4, 3, 5), (6, 0, 2), (6, 1, 2), (6, 2, 2),
        (7, 0, 3), (7, 1, 3), (7, 2, 3), (6, 3, 2),
    ],
    5: [
        (5, 0, 4), (5, 0, 6), (5, 1, 4), (5, 1, 6), (5, 2, 4), (5, 2, 6), (4, 0, 6), (6, 0, 4),
        (4, 1, 6), (6, 1, 4), (4, 2, 6), (6, 2, 4), (5, 3, 6), (7, 0, 4), (4, 3, 6), (7, 1, 4),
        (7, 2, 4), (6, 3, 4), (5, 3, 4), (7, 3, 4),
    ],
    6: [
        (6, 0, 5), (6, 0, 7), (6, 1, 5), (6, 1, 7), (6, 2, 5), (6, 2, 7), (5, 0, 7), (7, 0, 5),
        (5, 1, 7), (7, 1, 5), (5, 2, 7), (7, 2, 5), (4, 0, 7), (6, 3, 5), (4, 1, 7), (7, 3, 5),
        (4, 2, 7), (5, 3, 7), (6, 3, 7), (4, 3, 7),
    ],
    7: [
        (7, 0, 6), (7, 1, 6), (7, 2, 6), (7, 3, 2), (7, 3, 6), (5, 0, 1), (5, 1, 1), (5, 2, 1),
        (4, 0, 0), (4, 1, 0), (4, 2, 0), (5, 3, 1),
    ],
}
HOPS = (3,)
CROSSING = sorted({(z, t) for z, sends in ORDER.items() for _, _, t in sends if z // N_ROW != t // N_ROW})
MOST = 21
PIECES = 4
LAG = 3


def basis():
    n = np.arange(CHANNELS)[:, None]
    k = np.arange(BAND)[None, :]
    angle = ((n * k) % CHANNELS).astype(np.float32) * np.float32(2.0 * math.pi / CHANNELS)
    cos, sin = np.cos(angle), np.sin(angle)
    return np.stack([np.concatenate([cos, -sin] * 2, 1), np.concatenate([sin, cos] * 2, 1)])


def column_of(cols, ch):
    return jnp.concatenate(
        [cols[:, t, ch].reshape(N_ROW * GROUPS * ANT, 2 * WIDTH) for t in range(CHUNKS)], axis=1
    )


def left_of(rows, ch, slot):
    here = [rows[slot, t, ch].reshape(GROUPS * ANT, 2 * WIDTH) for t in range(CHUNKS)]
    turned = [jnp.concatenate([x[:, WIDTH:], -x[:, :WIDTH]], axis=1) for x in here]
    return jnp.concatenate([jnp.concatenate(here, axis=1), jnp.concatenate(turned, axis=1)], axis=0)


def fill(out, left, column):
    power = lax.dot_general(left, column, (((1,), (1,)), ((), ())), preferred_element_type=jnp.float32)
    power = power * (1.0 / math.sqrt(SPECTRA))
    for part in range(2):
        for g in range(N_ROW):
            out[part, pl.ds(g, 128, stride=N_ROW), :] = power[part * 128 : (part + 1) * 128, g * 128 : (g + 1) * 128]


def gather_kernel(
    volt, waves, window, flags, rows, cols, near,
    vbuf, wbuf, fbuf, kbuf, table, gbuf, cbuf, tbuf, sbuf, hop,
    volt_sem, small_sem, turn_send, turn_recv, own_sem, line_send, row_recv, col_recv, swap_send, hop_recv, answer,
):
    k = lax.axis_index("chan")
    r = lax.axis_index("row")
    c = lax.axis_index("col")
    hi, core = c // 2, c % 2
    plane = hi * N_ROW + r
    other = 1 - core

    def at_plane(z):
        return (k, z % N_ROW, (z // N_ROW) * 2 + core)

    mate = (k, r, hi * 2 + other)

    small = [
        pltpu.make_async_copy(window, fbuf, small_sem.at[0]),
        pltpu.make_async_copy(waves, wbuf, small_sem.at[1]),
        pltpu.make_async_copy(flags, kbuf, small_sem.at[2]),
    ]
    reads = []
    for chunk in range(CHUNKS):
        lo, up = BOUNDS[chunk], BOUNDS[chunk + 1]
        reads.append(pltpu.make_async_copy(
            volt.at[:, pl.ds(lo, up - lo)], vbuf.at[:, pl.ds(lo, up - lo)], volt_sem.at[chunk]
        ))
    small[0].start()
    small[1].start()
    reads[0].start()
    small[2].start()

    barrier = pltpu.get_barrier_semaphore()

    def greet(d, carry):
        pl.semaphore_signal(barrier, inc=1, device_id=((k + d) % GROUPS, r, c), device_id_type=MESH)
        return carry

    lax.fori_loop(1, GROUPS, greet, 0)
    for offset in range(1, N_ROW):
        pl.semaphore_signal(barrier, inc=1, device_id=(k, (r + offset) % N_ROW, c), device_id_type=MESH)
    pl.semaphore_signal(barrier, inc=1, device_id=mate, device_id_type=MESH)

    small[0].wait()
    weight = fbuf[...] * (1.0 / math.sqrt(TAPS * CHANNELS))
    weight = jnp.concatenate([weight, weight], axis=0).T
    small[1].wait()
    lane = lax.broadcasted_iota(jnp.int32, (CHANNELS, 128), 1)
    for half in range(2):
        scale = jnp.where(lane < 64, weight[:, 2 * half : 2 * half + 1], weight[:, 2 * half + 1 : 2 * half + 2])
        for part in range(2):
            table[part, :, half * 128 : (half + 1) * 128] = (wbuf[part] * scale).astype(jnp.bfloat16)

    def channelise(chunk):
        lo, up = BOUNDS[chunk], BOUNDS[chunk + 1]
        reads[chunk].wait()
        if chunk == 0:
            for copy in reads[1:]:
                copy.start()
        block = (min(up + 1, PADDED) - lo) // 2
        for f0 in (lo, lo + block):
            v0 = vbuf[0, f0 : f0 + block].reshape(block * ANT, CHANNELS)
            v1 = vbuf[1, f0 : f0 + block].reshape(block * ANT, CHANNELS)
            g = jnp.dot(v0, table[0], preferred_element_type=jnp.float32)
            g = g + jnp.dot(v1, table[1], preferred_element_type=jnp.float32)
            gbuf[f0 * ANT : (f0 + block) * ANT] = g

        s0 = chunk * WIDTH * ANT
        size = WIDTH * ANT
        pair = gbuf[pl.ds(s0, size + ANT), 0:128] + gbuf[pl.ds(s0 + 2 * ANT, size + ANT), 128:256]
        cbuf[...] = pair[:size] + pltpu.roll(pair[ANT:], 64, 1)
        for a in range(ANT):
            turned = cbuf[pl.ds(a, WIDTH, stride=ANT), :].T
            both = jnp.concatenate([turned[0:BAND], turned[BAND : 2 * BAND]], axis=1)
            tbuf[pl.ds(a, BAND, stride=ANT), :] = both
        if chunk == 0:
            small[2].wait()
        kept = kbuf[:, chunk * WIDTH : (chunk + 1) * WIDTH].astype(jnp.float32)
        kept = jnp.concatenate([kept, kept], axis=1)
        spectra = tbuf[...].reshape(GROUPS, PER, ANT, 2 * WIDTH) * kept[None, None]
        sbuf[chunk] = spectra.astype(jnp.bfloat16)

    def turn(chunk):
        def send(d, carry):
            j = (k + d) % GROUPS
            pltpu.make_async_remote_copy(
                src_ref=sbuf.at[chunk, j],
                dst_ref=rows.at[c, chunk, :, k],
                send_sem=turn_send.at[chunk],
                recv_sem=turn_recv.at[chunk],
                device_id=(j, r, c),
                device_id_type=MESH,
            ).start()
            return carry

        lax.fori_loop(1, GROUPS, send, 0)
        pltpu.make_async_copy(sbuf.at[chunk, k], rows.at[c, chunk, :, k], turn_recv.at[chunk]).start()

    def turned(chunk):
        whole = rows.at[c, chunk]
        pltpu.make_async_copy(whole, whole, turn_recv.at[chunk]).wait()

    def swap(chunk, slot, index):
        copy = pltpu.make_async_remote_copy(
            src_ref=rows.at[slot, chunk],
            dst_ref=rows.at[slot, chunk],
            send_sem=swap_send.at[chunk, index],
            recv_sem=row_recv.at[chunk, slot],
            device_id=mate,
            device_id_type=MESH,
        )
        copy.start()
        return copy

    def line_copy(z, index):
        source, chunk, target = ORDER[z][index]
        line, place = source // N_ROW, source % N_ROW
        slot = line * 2 + core
        if source == z:
            src = rows.at[slot, chunk]
        elif line == z // N_ROW:
            src = cols.at[place, chunk]
        else:
            src = hop.at[HOPS.index(chunk)]
        if line == target // N_ROW:
            dst, sem = cols.at[place, chunk], col_recv.at[chunk, place]
        elif target == (source + N_ROW) % PLANES:
            dst, sem = rows.at[slot, chunk], row_recv.at[chunk, slot]
        else:
            dst, sem = hop.at[HOPS.index(chunk)], hop_recv.at[HOPS.index(chunk)]
        return pltpu.make_async_remote_copy(
            src_ref=src, dst_ref=dst, send_sem=line_send.at[index], recv_sem=sem,
            device_id=at_plane(target), device_id_type=MESH,
        )

    def wait_hop(chunk):
        piece = hop.at[HOPS.index(chunk)]
        pltpu.make_async_copy(piece, piece, hop_recv.at[HOPS.index(chunk)]).wait()

    def wait_col(chunk, source):
        piece = cols.at[source, chunk]
        pltpu.make_async_copy(piece, piece, col_recv.at[chunk, source]).wait()

    def wait_row(chunk, slot):
        piece = rows.at[slot, chunk]
        pltpu.make_async_copy(piece, piece, row_recv.at[chunk, slot]).wait()

    far = (1 - hi) * 2 + core

    def each_plane(act):
        for z in range(PLANES):
            @pl.when(plane == z)
            def _(z=z):
                act(z)

    def enter(z):
        near = GROUPS - 1 + N_ROW - 1 + 1
        partners = sorted({pair[0] + pair[1] - z for pair in CROSSING if z in pair})
        if z < N_ROW:
            pl.semaphore_wait(barrier, near)
            for partner in partners:
                pl.semaphore_signal(barrier, inc=1, device_id=at_plane(partner), device_id_type=MESH)
        else:
            pl.semaphore_wait(barrier, near + len(partners))
            for sender, target in CROSSING:
                if target == z:
                    pl.semaphore_signal(answer, inc=1, device_id=at_plane(sender), device_id_type=MESH)

    def first_need(z, chunk):
        for index, (source, step, _) in enumerate(ORDER[z]):
            if (source == z and step >= chunk) or (source != z and chunk < CHUNKS):
                return index
        return len(ORDER[z])

    def send_step(z, chunk):
        for index in range(first_need(z, chunk), first_need(z, chunk + 1)):
            source, step, _ = ORDER[z][index]
            if source != z and all(item[:2] != (source, step) for item in ORDER[z][:index]):
                if source // N_ROW == z // N_ROW:
                    wait_col(step, source % N_ROW)
                else:
                    wait_hop(step)
            crossing = [i for i, item in enumerate(ORDER[z]) if item[2] // N_ROW != z // N_ROW]
            if z < N_ROW and crossing and index == crossing[0]:
                pl.semaphore_wait(answer, len([pair for pair in CROSSING if pair[0] == z]))
            line_copy(z, index).start()
        if chunk == CHUNKS - 1:
            relayed = [item[:2] for item in ORDER[z]]
            for source in range(z // N_ROW * N_ROW, (z // N_ROW + 1) * N_ROW):
                for step in range(CHUNKS):
                    if source != z and (source, step) not in relayed:
                        wait_col(step, source % N_ROW)

    swaps, owns = [], []

    def sends(chunk):
        turned(chunk)
        swaps.append(swap(chunk, c, 0))
        own = pltpu.make_async_copy(rows.at[c, chunk], cols.at[r, chunk], own_sem.at[chunk])
        own.start()
        owns.append(own)
        each_plane(lambda z: send_step(z, chunk))

    for chunk in range(CHUNKS):
        channelise(chunk)
        if chunk == 0:
            each_plane(enter)
        turn(chunk)
        if chunk >= LAG:
            sends(chunk - LAG)
    for chunk in range(CHUNKS - LAG, CHUNKS):
        sends(chunk)
    for copy in owns:
        copy.wait()
    for chunk in range(CHUNKS):
        wait_row(chunk, hi * 2 + other)
    for chunk in range(CHUNKS):
        if chunk < PER:
            ch = chunk
            column = column_of(cols, ch)
            for piece in range(PIECES // 2):
                fill(near.at[ch, piece], left_of(rows, ch, hi * 2 + piece), column)
        wait_row(chunk, far)
        swaps.append(swap(chunk, far, 1))
    for chunk in range(CHUNKS):
        sent = sbuf.at[chunk, pl.ds(0, GROUPS - 1)]
        pltpu.make_async_copy(sent, sent, turn_send.at[chunk]).wait()
    for copy in swaps:
        copy.wait_send()

    def finish(z):
        for index in range(len(ORDER[z])):
            line_copy(z, index).wait_send()

    each_plane(finish)
    for chunk in range(CHUNKS):
        wait_row(chunk, (1 - hi) * 2 + other)


def gather(volt, window, flags):
    shape = jax.ShapeDtypeStruct((N_ROW, CHUNKS, PER, GROUPS, ANT, 2 * WIDTH), jnp.bfloat16)
    anywhere = pl.BlockSpec(memory_space=pltpu.HBM)
    inside = pl.BlockSpec(memory_space=pltpu.VMEM)
    return pl.pallas_call(
        gather_kernel,
        out_shape=(shape, shape, jax.ShapeDtypeStruct((PER, PIECES // 2, 2, 128 * N_ROW, 128), jnp.float32)),
        in_specs=[anywhere] * 4,
        out_specs=(inside, inside, inside),
        scratch_shapes=[
            pltpu.VMEM((2, PADDED, ANT, CHANNELS), jnp.bfloat16),
            pltpu.VMEM((2, CHANNELS, 128), jnp.float32),
            pltpu.VMEM((TAPS, CHANNELS), jnp.float32),
            pltpu.VMEM((ANT, SPECTRA), jnp.int32),
            pltpu.VMEM((2, CHANNELS, 256), jnp.bfloat16),
            pltpu.VMEM((PADDED * ANT, 256), jnp.float32),
            pltpu.VMEM((WIDTH * ANT, 128), jnp.float32),
            pltpu.VMEM((BAND * ANT, 2 * WIDTH), jnp.float32),
            pltpu.VMEM((CHUNKS, GROUPS, PER, ANT, 2 * WIDTH), jnp.bfloat16),
            pltpu.VMEM((max(1, len(HOPS)), PER, GROUPS, ANT, 2 * WIDTH), jnp.bfloat16),
            pltpu.SemaphoreType.DMA((CHUNKS,)),
            pltpu.SemaphoreType.DMA((3,)),
            pltpu.SemaphoreType.DMA((CHUNKS,)),
            pltpu.SemaphoreType.DMA((CHUNKS,)),
            pltpu.SemaphoreType.DMA((CHUNKS,)),
            pltpu.SemaphoreType.DMA((MOST,)),
            pltpu.SemaphoreType.DMA((CHUNKS, N_ROW)),
            pltpu.SemaphoreType.DMA((CHUNKS, N_ROW)),
            pltpu.SemaphoreType.DMA((CHUNKS, 2)),
            pltpu.SemaphoreType.DMA((max(1, len(HOPS)),)),
            pltpu.SemaphoreType.REGULAR,
        ],
        compiler_params=pltpu.CompilerParams(
            collective_id=0, has_side_effects=True, vmem_limit_bytes=40 * 1024 * 1024
        ),
        name="gather",
    )(*(pltpu.with_memory_space_constraint(x, pltpu.HBM) for x in (volt, jnp.asarray(basis()), window, flags)))


def power_kernel(rows, cols, near, out, held, near_sem, sem):
    hi = lax.axis_index("col") // 2
    copies = []

    def write(src, ch, slot, where):
        lines = pl.ds(pl.multiple_of(slot * 128 * N_ROW, 128 * N_ROW), 128 * N_ROW)
        copy = pltpu.make_async_copy(src, out.at[:, ch, lines], where)
        copy.start()
        copies.append(copy)

    for ch in range(PER):
        for piece in range(PIECES // 2):
            write(near.at[ch, piece], ch, hi * 2 + piece, near_sem.at[ch, piece])
    for ch in range(PER):
        column = column_of(cols, ch)
        for piece in range(PIECES // 2):
            slot = (1 - hi) * 2 + piece
            fill(held.at[ch, piece], left_of(rows, ch, slot), column)
            write(held.at[ch, piece], ch, slot, sem.at[ch, piece])
    for copy in copies:
        copy.wait()


def power(rows, cols, near):
    inside = pl.BlockSpec(memory_space=pltpu.VMEM)
    return pl.pallas_call(
        power_kernel,
        out_shape=jax.ShapeDtypeStruct((2, PER, 512 * N_ROW, 128), jnp.float32),
        in_specs=[inside, inside, inside],
        out_specs=pl.BlockSpec(memory_space=pltpu.HBM),
        scratch_shapes=[
            pltpu.VMEM((PER, PIECES // 2, 2, 128 * N_ROW, 128), jnp.float32),
            pltpu.SemaphoreType.DMA((PER, PIECES // 2)),
            pltpu.SemaphoreType.DMA((PER, PIECES // 2)),
        ],
        compiler_params=pltpu.CompilerParams(vmem_limit_bytes=40 * 1024 * 1024),
        name="power",
    )(rows, cols, near)


def on_device(voltages, fir_window, flags):
    frames = voltages.reshape(2, ANT, FRAMES, CHANNELS).transpose(0, 2, 1, 3)
    rows, cols, near = gather(frames, fir_window, flags)
    return power(rows, cols, near).reshape(2, PER, 512, N_ROW, 128)


def solution(mesh):
    return jax.shard_map(
        on_device,
        mesh=mesh,
        in_specs=(P(None, ("row", "col", "chan"), None), P(), P(("row", "col", "chan"), None)),
        out_specs=P(None, "chan", "row", None, "col"),
        check_vma=False,
    )
```

```python
import math

import jax
import jax.numpy as jnp
import numpy as np
from jax import lax
from jax.experimental import pallas as pl
from jax.experimental.pallas import tpu as pltpu
from jax.sharding import PartitionSpec as P

MESH = pl.DeviceIdType.MESH

CHANNELS = 1024
TAPS = 4
BAND = 32
SPECTRA = 256
FRAMES = SPECTRA + TAPS - 1
ANT = 8
GROUPS = 16
PER = BAND // GROUPS
N_ROW = 4
PLANES = 8
CHUNKS = 4
WIDTH = SPECTRA // CHUNKS
BOUNDS = (0, 68, 132, 196, FRAMES)
PADDED = 260

ORDER = {
    0: [
        (0, 0, 1), (0, 1, 1), (0, 2, 1), (0, 3, 1), (2, 0, 6), (2, 1, 6), (2, 2, 6), (3, 0, 7),
        (3, 1, 7), (3, 2, 7), (2, 3, 6), (3, 3, 7),
    ],
    1: [
        (1, 0, 0), (1, 0, 2), (1, 1, 0), (1, 1, 2), (1, 2, 0), (1, 2, 2), (0, 0, 2), (2, 0, 0),
        (0, 1, 2), (2, 1, 0), (0, 2, 2), (2, 2, 0), (1, 3, 2), (3, 0, 0), (0, 3, 2), (3, 1, 0),
        (3, 2, 0), (2, 3, 0), (3, 3, 0), (4, 3, 0), (1, 3, 0),
    ],
    2: [
        (2, 0, 1), (2, 0, 3), (2, 1, 1), (2, 1, 3), (2, 2, 1), (2, 2, 3), (1, 0, 3), (3, 0, 1),
        (1, 1, 3), (3, 1, 1), (1, 2, 3), (3, 2, 1), (0, 0, 3), (2, 3, 1), (0, 1, 3), (3, 3, 1),
        (0, 2, 3), (1, 3, 3), (0, 3, 3), (7, 3, 3), (2, 3, 3),
    ],
    3: [
        (3, 0, 2), (3, 1, 2), (3, 2, 2), (3, 3, 2), (1, 0, 5), (1, 1, 5), (1, 2, 5), (0, 0, 4),
        (0, 1, 4), (0, 2, 4), (1, 3, 5), (0, 3, 4),
    ],
    4: [
        (4, 0, 5), (4, 1, 5), (4, 2, 5), (4, 3, 1), (4, 3, 5), (6, 0, 2), (6, 1, 2), (6, 2, 2),
        (7, 0, 3), (7, 1, 3), (7, 2, 3), (6, 3, 2),
    ],
    5: [
        (5, 0, 4), (5, 0, 6), (5, 1, 4), (5, 1, 6), (5, 2, 4), (5, 2, 6), (4, 0, 6), (6, 0, 4),
        (4, 1, 6), (6, 1, 4), (4, 2, 6), (6, 2, 4), (5, 3, 6), (7, 0, 4), (4, 3, 6), (7, 1, 4),
        (7, 2, 4), (6, 3, 4), (5, 3, 4), (7, 3, 4),
    ],
    6: [
        (6, 0, 5), (6, 0, 7), (6, 1, 5), (6, 1, 7), (6, 2, 5), (6, 2, 7), (5, 0, 7), (7, 0, 5),
        (5, 1, 7), (7, 1, 5), (5, 2, 7), (7, 2, 5), (4, 0, 7), (6, 3, 5), (4, 1, 7), (7, 3, 5),
        (4, 2, 7), (5, 3, 7), (6, 3, 7), (4, 3, 7),
    ],
    7: [
        (7, 0, 6), (7, 1, 6), (7, 2, 6), (7, 3, 2), (7, 3, 6), (5, 0, 1), (5, 1, 1), (5, 2, 1),
        (4, 0, 0), (4, 1, 0), (4, 2, 0), (5, 3, 1),
    ],
}
HOPS = (3,)
CROSSING = sorted({(z, t) for z, sends in ORDER.items() for _, _, t in sends if z // N_ROW != t // N_ROW})
MOST = 21
PIECES = 4
LAG = 3


def basis():
    n = np.arange(CHANNELS)[:, None]
    k = np.arange(BAND)[None, :]
    angle = ((n * k) % CHANNELS).astype(np.float32) * np.float32(2.0 * math.pi / CHANNELS)
    cos, sin = np.cos(angle), np.sin(angle)
    return np.stack([np.concatenate([cos, -sin] * 2, 1), np.concatenate([sin, cos] * 2, 1)])


def column_of(cols, ch):
    return jnp.concatenate(
        [cols[:, t, ch].reshape(N_ROW * GROUPS * ANT, 2 * WIDTH) for t in range(CHUNKS)], axis=1
    )


def left_of(rows, ch, slot):
    here = [rows[slot, t, ch].reshape(GROUPS * ANT, 2 * WIDTH) for t in range(CHUNKS)]
    turned = [jnp.concatenate([x[:, WIDTH:], -x[:, :WIDTH]], axis=1) for x in here]
    return jnp.concatenate([jnp.concatenate(here, axis=1), jnp.concatenate(turned, axis=1)], axis=0)


def fill(out, left, column):
    power = lax.dot_general(left, column, (((1,), (1,)), ((), ())), preferred_element_type=jnp.float32)
    power = power * (1.0 / math.sqrt(SPECTRA))
    for part in range(2):
        for g in range(N_ROW):
            out[part, pl.ds(g, 128, stride=N_ROW), :] = power[part * 128 : (part + 1) * 128, g * 128 : (g + 1) * 128]


def gather_kernel(
    volt, waves, window, flags, rows, cols, near,
    vbuf, wbuf, fbuf, kbuf, table, gbuf, cbuf, tbuf, sbuf, hop,
    volt_sem, small_sem, turn_send, turn_recv, own_sem, line_send, row_recv, col_recv, swap_send, hop_recv, answer,
):
    k = lax.axis_index("chan")
    r = lax.axis_index("row")
    c = lax.axis_index("col")
    hi, core = c // 2, c % 2
    plane = hi * N_ROW + r
    other = 1 - core

    def at_plane(z):
        return (k, z % N_ROW, (z // N_ROW) * 2 + core)

    mate = (k, r, hi * 2 + other)

    small = [
        pltpu.make_async_copy(window, fbuf, small_sem.at[0]),
        pltpu.make_async_copy(waves, wbuf, small_sem.at[1]),
        pltpu.make_async_copy(flags, kbuf, small_sem.at[2]),
    ]
    reads = []
    for chunk in range(CHUNKS):
        lo, up = BOUNDS[chunk], BOUNDS[chunk + 1]
        reads.append(pltpu.make_async_copy(
            volt.at[:, pl.ds(lo, up - lo)], vbuf.at[:, pl.ds(lo, up - lo)], volt_sem.at[chunk]
        ))
    small[0].start()
    small[1].start()
    reads[0].start()
    small[2].start()

    barrier = pltpu.get_barrier_semaphore()

    def greet(d, carry):
        pl.semaphore_signal(barrier, inc=1, device_id=((k + d) % GROUPS, r, c), device_id_type=MESH)
        return carry

    lax.fori_loop(1, GROUPS, greet, 0)
    for offset in range(1, N_ROW):
        pl.semaphore_signal(barrier, inc=1, device_id=(k, (r + offset) % N_ROW, c), device_id_type=MESH)
    pl.semaphore_signal(barrier, inc=1, device_id=mate, device_id_type=MESH)

    small[0].wait()
    weight = fbuf[...] * (1.0 / math.sqrt(TAPS * CHANNELS))
    weight = jnp.concatenate([weight, weight], axis=0).T
    small[1].wait()
    lane = lax.broadcasted_iota(jnp.int32, (CHANNELS, 128), 1)
    for half in range(2):
        scale = jnp.where(lane < 64, weight[:, 2 * half : 2 * half + 1], weight[:, 2 * half + 1 : 2 * half + 2])
        for part in range(2):
            table[part, :, half * 128 : (half + 1) * 128] = (wbuf[part] * scale).astype(jnp.bfloat16)

    def channelise(chunk):
        lo, up = BOUNDS[chunk], BOUNDS[chunk + 1]
        reads[chunk].wait()
        if chunk == 0:
            for copy in reads[1:]:
                copy.start()
        block = (min(up + 1, PADDED) - lo) // 2
        for f0 in (lo, lo + block):
            v0 = vbuf[0, f0 : f0 + block].reshape(block * ANT, CHANNELS)
            v1 = vbuf[1, f0 : f0 + block].reshape(block * ANT, CHANNELS)
            g = jnp.dot(v0, table[0], preferred_element_type=jnp.float32)
            g = g + jnp.dot(v1, table[1], preferred_element_type=jnp.float32)
            gbuf[f0 * ANT : (f0 + block) * ANT] = g

        s0 = chunk * WIDTH * ANT
        size = WIDTH * ANT
        pair = gbuf[pl.ds(s0, size + ANT), 0:128] + gbuf[pl.ds(s0 + 2 * ANT, size + ANT), 128:256]
        cbuf[...] = pair[:size] + pltpu.roll(pair[ANT:], 64, 1)
        for a in range(ANT):
            turned = cbuf[pl.ds(a, WIDTH, stride=ANT), :].T
            both = jnp.concatenate([turned[0:BAND], turned[BAND : 2 * BAND]], axis=1)
            tbuf[pl.ds(a, BAND, stride=ANT), :] = both
        if chunk == 0:
            small[2].wait()
        kept = kbuf[:, chunk * WIDTH : (chunk + 1) * WIDTH].astype(jnp.float32)
        kept = jnp.concatenate([kept, kept], axis=1)
        spectra = tbuf[...].reshape(GROUPS, PER, ANT, 2 * WIDTH) * kept[None, None]
        sbuf[chunk] = spectra.astype(jnp.bfloat16)

    def turn(chunk):
        def send(d, carry):
            j = (k + d) % GROUPS
            pltpu.make_async_remote_copy(
                src_ref=sbuf.at[chunk, j],
                dst_ref=rows.at[c, chunk, :, k],
                send_sem=turn_send.at[chunk],
                recv_sem=turn_recv.at[chunk],
                device_id=(j, r, c),
                device_id_type=MESH,
            ).start()
            return carry

        lax.fori_loop(1, GROUPS, send, 0)
        pltpu.make_async_copy(sbuf.at[chunk, k], rows.at[c, chunk, :, k], turn_recv.at[chunk]).start()

    def turned(chunk):
        whole = rows.at[c, chunk]
        pltpu.make_async_copy(whole, whole, turn_recv.at[chunk]).wait()

    def swap(chunk, slot, index):
        copy = pltpu.make_async_remote_copy(
            src_ref=rows.at[slot, chunk],
            dst_ref=rows.at[slot, chunk],
            send_sem=swap_send.at[chunk, index],
            recv_sem=row_recv.at[chunk, slot],
            device_id=mate,
            device_id_type=MESH,
        )
        copy.start()
        return copy

    def line_copy(z, index):
        source, chunk, target = ORDER[z][index]
        line, place = source // N_ROW, source % N_ROW
        slot = line * 2 + core
        if source == z:
            src = rows.at[slot, chunk]
        elif line == z // N_ROW:
            src = cols.at[place, chunk]
        else:
            src = hop.at[HOPS.index(chunk)]
        if line == target // N_ROW:
            dst, sem = cols.at[place, chunk], col_recv.at[chunk, place]
        elif target == (source + N_ROW) % PLANES:
            dst, sem = rows.at[slot, chunk], row_recv.at[chunk, slot]
        else:
            dst, sem = hop.at[HOPS.index(chunk)], hop_recv.at[HOPS.index(chunk)]
        return pltpu.make_async_remote_copy(
            src_ref=src, dst_ref=dst, send_sem=line_send.at[index], recv_sem=sem,
            device_id=at_plane(target), device_id_type=MESH,
        )

    def wait_hop(chunk):
        piece = hop.at[HOPS.index(chunk)]
        pltpu.make_async_copy(piece, piece, hop_recv.at[HOPS.index(chunk)]).wait()

    def wait_col(chunk, source):
        piece = cols.at[source, chunk]
        pltpu.make_async_copy(piece, piece, col_recv.at[chunk, source]).wait()

    def wait_row(chunk, slot):
        piece = rows.at[slot, chunk]
        pltpu.make_async_copy(piece, piece, row_recv.at[chunk, slot]).wait()

    far = (1 - hi) * 2 + core

    def each_plane(act):
        for z in range(PLANES):
            @pl.when(plane == z)
            def _(z=z):
                act(z)

    def enter(z):
        near = GROUPS - 1 + N_ROW - 1 + 1
        partners = sorted({pair[0] + pair[1] - z for pair in CROSSING if z in pair})
        if z < N_ROW:
            pl.semaphore_wait(barrier, near)
            for partner in partners:
                pl.semaphore_signal(barrier, inc=1, device_id=at_plane(partner), device_id_type=MESH)
        else:
            pl.semaphore_wait(barrier, near + len(partners))
            for sender, target in CROSSING:
                if target == z:
                    pl.semaphore_signal(answer, inc=1, device_id=at_plane(sender), device_id_type=MESH)

    def first_need(z, chunk):
        for index, (source, step, _) in enumerate(ORDER[z]):
            if (source == z and step >= chunk) or (source != z and chunk < CHUNKS):
                return index
        return len(ORDER[z])

    def send_step(z, chunk):
        for index in range(first_need(z, chunk), first_need(z, chunk + 1)):
            source, step, _ = ORDER[z][index]
            if source != z and all(item[:2] != (source, step) for item in ORDER[z][:index]):
                if source // N_ROW == z // N_ROW:
                    wait_col(step, source % N_ROW)
                else:
                    wait_hop(step)
            crossing = [i for i, item in enumerate(ORDER[z]) if item[2] // N_ROW != z // N_ROW]
            if z < N_ROW and crossing and index == crossing[0]:
                pl.semaphore_wait(answer, len([pair for pair in CROSSING if pair[0] == z]))
            line_copy(z, index).start()
        if chunk == CHUNKS - 1:
            relayed = [item[:2] for item in ORDER[z]]
            for source in range(z // N_ROW * N_ROW, (z // N_ROW + 1) * N_ROW):
                for step in range(CHUNKS):
                    if source != z and (source, step) not in relayed:
                        wait_col(step, source % N_ROW)

    swaps, owns = [], []

    def sends(chunk):
        turned(chunk)
        last = chunk == CHUNKS - 1
        if not last:
            each_plane(lambda z: send_step(z, chunk))
        swaps.append(swap(chunk, c, 0))
        own = pltpu.make_async_copy(rows.at[c, chunk], cols.at[r, chunk], own_sem.at[chunk])
        own.start()
        owns.append(own)
        if last:
            each_plane(lambda z: send_step(z, chunk))

    for chunk in range(CHUNKS):
        channelise(chunk)
        if chunk == 0:
            each_plane(enter)
        turn(chunk)
        if chunk >= LAG:
            sends(chunk - LAG)
    for chunk in range(CHUNKS - LAG, CHUNKS):
        sends(chunk)
    for copy in owns:
        copy.wait()
    for chunk in range(CHUNKS):
        wait_row(chunk, hi * 2 + other)
    for chunk in range(CHUNKS):
        if chunk < PER:
            ch = chunk
            column = column_of(cols, ch)
            for piece in range(PIECES // 2):
                fill(near.at[ch, piece], left_of(rows, ch, hi * 2 + piece), column)
        wait_row(chunk, far)
        swaps.append(swap(chunk, far, 1))
    for chunk in range(CHUNKS):
        sent = sbuf.at[chunk, pl.ds(0, GROUPS - 1)]
        pltpu.make_async_copy(sent, sent, turn_send.at[chunk]).wait()
    for copy in swaps:
        copy.wait_send()

    def finish(z):
        for index in range(len(ORDER[z])):
            line_copy(z, index).wait_send()

    each_plane(finish)
    for chunk in range(CHUNKS):
        wait_row(chunk, (1 - hi) * 2 + other)


def gather(volt, window, flags):
    shape = jax.ShapeDtypeStruct((N_ROW, CHUNKS, PER, GROUPS, ANT, 2 * WIDTH), jnp.bfloat16)
    anywhere = pl.BlockSpec(memory_space=pltpu.HBM)
    inside = pl.BlockSpec(memory_space=pltpu.VMEM)
    return pl.pallas_call(
        gather_kernel,
        out_shape=(shape, shape, jax.ShapeDtypeStruct((PER, PIECES // 2, 2, 128 * N_ROW, 128), jnp.float32)),
        in_specs=[anywhere] * 4,
        out_specs=(inside, inside, inside),
        scratch_shapes=[
            pltpu.VMEM((2, PADDED, ANT, CHANNELS), jnp.bfloat16),
            pltpu.VMEM((2, CHANNELS, 128), jnp.float32),
            pltpu.VMEM((TAPS, CHANNELS), jnp.float32),
            pltpu.VMEM((ANT, SPECTRA), jnp.int32),
            pltpu.VMEM((2, CHANNELS, 256), jnp.bfloat16),
            pltpu.VMEM((PADDED * ANT, 256), jnp.float32),
            pltpu.VMEM((WIDTH * ANT, 128), jnp.float32),
            pltpu.VMEM((BAND * ANT, 2 * WIDTH), jnp.float32),
            pltpu.VMEM((CHUNKS, GROUPS, PER, ANT, 2 * WIDTH), jnp.bfloat16),
            pltpu.VMEM((max(1, len(HOPS)), PER, GROUPS, ANT, 2 * WIDTH), jnp.bfloat16),
            pltpu.SemaphoreType.DMA((CHUNKS,)),
            pltpu.SemaphoreType.DMA((3,)),
            pltpu.SemaphoreType.DMA((CHUNKS,)),
            pltpu.SemaphoreType.DMA((CHUNKS,)),
            pltpu.SemaphoreType.DMA((CHUNKS,)),
            pltpu.SemaphoreType.DMA((MOST,)),
            pltpu.SemaphoreType.DMA((CHUNKS, N_ROW)),
            pltpu.SemaphoreType.DMA((CHUNKS, N_ROW)),
            pltpu.SemaphoreType.DMA((CHUNKS, 2)),
            pltpu.SemaphoreType.DMA((max(1, len(HOPS)),)),
            pltpu.SemaphoreType.REGULAR,
        ],
        compiler_params=pltpu.CompilerParams(
            collective_id=0, has_side_effects=True, vmem_limit_bytes=40 * 1024 * 1024
        ),
        name="gather",
    )(*(pltpu.with_memory_space_constraint(x, pltpu.HBM) for x in (volt, jnp.asarray(basis()), window, flags)))


def power_kernel(rows, cols, near, out, held, near_sem, sem):
    hi = lax.axis_index("col") // 2
    copies = []

    def write(src, ch, slot, where):
        lines = pl.ds(pl.multiple_of(slot * 128 * N_ROW, 128 * N_ROW), 128 * N_ROW)
        copy = pltpu.make_async_copy(src, out.at[:, ch, lines], where)
        copy.start()
        copies.append(copy)

    for ch in range(PER):
        for piece in range(PIECES // 2):
            write(near.at[ch, piece], ch, hi * 2 + piece, near_sem.at[ch, piece])
    for ch in range(PER):
        column = column_of(cols, ch)
        for piece in range(PIECES // 2):
            slot = (1 - hi) * 2 + piece
            fill(held.at[ch, piece], left_of(rows, ch, slot), column)
            write(held.at[ch, piece], ch, slot, sem.at[ch, piece])
    for copy in copies:
        copy.wait()


def power(rows, cols, near):
    inside = pl.BlockSpec(memory_space=pltpu.VMEM)
    return pl.pallas_call(
        power_kernel,
        out_shape=jax.ShapeDtypeStruct((2, PER, 512 * N_ROW, 128), jnp.float32),
        in_specs=[inside, inside, inside],
        out_specs=pl.BlockSpec(memory_space=pltpu.HBM),
        scratch_shapes=[
            pltpu.VMEM((PER, PIECES // 2, 2, 128 * N_ROW, 128), jnp.float32),
            pltpu.SemaphoreType.DMA((PER, PIECES // 2)),
            pltpu.SemaphoreType.DMA((PER, PIECES // 2)),
        ],
        compiler_params=pltpu.CompilerParams(vmem_limit_bytes=40 * 1024 * 1024),
        name="power",
    )(rows, cols, near)


def on_device(voltages, fir_window, flags):
    frames = voltages.reshape(2, ANT, FRAMES, CHANNELS).transpose(0, 2, 1, 3)
    rows, cols, near = gather(frames, fir_window, flags)
    return power(rows, cols, near).reshape(2, PER, 512, N_ROW, 128)


def solution(mesh):
    return jax.shard_map(
        on_device,
        mesh=mesh,
        in_specs=(P(None, ("row", "col", "chan"), None), P(), P(("row", "col", "chan"), None)),
        out_specs=P(None, "chan", "row", None, "col"),
        check_vma=False,
    )
```
